256 devices in a mesh: tok: 8 (over z_lo, core), row: 4 (over x), col: 8 (over z_hi, y).
Axes of the slice: x: 4, y: 4, z: 8 (z_hi: 2, z_lo: 4; z = z_hi * 4 + z_lo), core: 2. Of those that a mesh axis runs over, the one named last changes fastest.
Arguments:
- hidden: bfloat16 [4096, 5120], P('tok', ('row', 'col')), may hold values from -6 to 6
- gains: float32 [8, 5120], P('tok', ('row', 'col')), may hold values from 0.25 to 1.75
- weights: bfloat16 [8, 5120, 2048], P('tok', 'row', 'col'), may hold values from -6 to 6
- lengths: int32 [8], replicated, may hold values from 1 to 512, 2304 in all
Outputs:
- merged: float32 [5120, 2048], P(('row', 'tok'), 'col')
The draws below stay inside these ranges and needn't reach their ends.
Inputs may be any that keep to these rules, and one draw needn't show every extreme that they name: The largest entry of lengths is exactly 512.
All inputs are finite; a program needn't handle non-finite values.
Results may differ from the reference program's by a relative error of at most 0.0054.
Values may be sent and summed in bfloat16 or wider, within the bound.
A program may use at most 64 MiB of HBM per device.

```python
import math
import jax
import jax.numpy as jnp
import numpy as np
from jax import lax

D = 5120
OUT = 2048
CAP = 512
ITERS = 4
MODELS = 8
TOKENS = 4096


def block_levels(stream_key, dims, shards, smallest, top_value):
    level, own = 1.0, jax.random.fold_in(stream_key, 6)
    for position, blocks in shards:
        heights = jnp.exp(jax.random.uniform(jax.random.fold_in(own, position), (blocks,), jnp.float32, smallest / len(shards), top_value / len(shards)))
        level = level * jnp.repeat(heights, dims[position] // blocks).reshape([-1 if axis == position else 1 for axis in range(len(dims))])
    return level


def split_up(count, total, limit, lean):
    weights = [(1 << 20) // math.isqrt(rank ** lean) + 1 for rank in range(2, count + 1)]
    rest, given = total - limit - (count - 1), [1] * (count - 1)
    while rest > 0:
        movable = [i for i in range(count - 1) if given[i] < limit]
        mass, left = sum([weights[i] for i in movable]), rest
        for i in movable:
            more = min(limit - given[i], max(1, left * weights[i] // mass), rest)
            given[i] = given[i] + more
            rest = rest - more
    return np.array([limit] + given)


def ragged_sizes(stream_key, count, total, bound, skew):
    if count == 2:
        one = jax.random.randint(stream_key, (), max(1, total - bound), min(bound, total - 1) + 1)
        return jnp.stack([one, total - one])
    sizes = jnp.asarray(split_up(count, total, bound, skew), jnp.int32)
    twos = (count - 1) // 2
    source_of, sink = sizes[1:1 + 2 * twos:2], sizes[2:2 + 2 * twos:2]
    margin = jnp.minimum(source_of - 1, bound - sink)
    shifted = jax.random.randint(jax.random.fold_in(stream_key, 1), (twos,), 0, 1 << 20) % (margin + 1)
    sizes = sizes.at[1:1 + 2 * twos:2].set(source_of - shifted).at[2:2 + 2 * twos:2].set(sink + shifted)
    return sizes[jax.random.permutation(jax.random.fold_in(stream_key, 2), count)]


def centred(key, extent, spread, most, split=(), held_as=jnp.bfloat16):
    drawn = spread * jax.random.normal(key, extent, jnp.float32)
    if split:
        drawn = drawn * block_levels(key, extent, split, -0.22, 0.18)
    return jnp.clip(drawn, -most, most).astype(held_as)


def setup_inputs(seed: int = 0) -> dict:
    key_of = jax.random.split(jax.random.key(seed), 5)
    return {
        "hidden": centred(key_of[0], (TOKENS, D), 1.0, 6.0, ((0, 8), (1, 32))),
        "gains": jnp.clip(1.0 + 0.15 * jax.random.normal(key_of[1], (MODELS, D), jnp.float32), 0.25, 1.75),
        "weights": centred(key_of[2], (MODELS, D, OUT), 1.0, 6.0, ((0, 8), (1, 4), (2, 8))),
        "lengths": ragged_sizes(key_of[3], MODELS, (MODELS + 1) * CAP // 2, CAP, 2).astype(jnp.int32),
    }


MIXING = 0.9
EPSILON = 1e-06

def reference(hidden, gains, weights, lengths):
    positions = jnp.arange(CAP, dtype=jnp.int32)
    tokens_all = hidden.astype(jnp.float32).reshape(MODELS, CAP, D)
    inverse_rms = lax.rsqrt(lax.optimization_barrier(jnp.sum(tokens_all * tokens_all, axis=2)) / D + EPSILON)
    live_mask = (positions[None, :] < lengths[:, None]).astype(jnp.float32)
    normed = (tokens_all * (inverse_rms * live_mask)[:, :, None] * gains[:, None, :]).astype(jnp.bfloat16)
    gram = jnp.zeros((D, D), jnp.float32)
    right = jnp.zeros((D, OUT), jnp.float32)
    for model in range(MODELS):
        block_model = normed[model]
        gram = gram + jnp.dot(block_model.T, block_model, preferred_element_type=jnp.float32)
        outputs = jnp.dot(block_model, weights[model], preferred_element_type=jnp.float32).astype(jnp.bfloat16)
        squared = lax.optimization_barrier(jnp.sum(jnp.square(block_model.astype(jnp.float32)), axis=0))
        cross_term = jnp.dot(block_model.T, outputs, preferred_element_type=jnp.float32)
        right = right + (MIXING * cross_term + (1.0 - MIXING) * squared[:, None] * weights[model].astype(jnp.float32))
    diagonal = jnp.diagonal(gram)

    def operate(direction):
        product = jnp.dot(gram, direction, precision=lax.Precision.HIGHEST)
        return MIXING * product + (1.0 - MIXING) * diagonal[:, None] * direction
    merged = jnp.zeros((D, OUT), jnp.float32)
    residual = right
    direction = right
    norm_now = lax.optimization_barrier(jnp.sum(residual * residual, axis=0))
    for step in range(ITERS):
        image = operate(direction)
        step_size = norm_now / lax.optimization_barrier(jnp.sum(direction * image, axis=0))
        merged = merged + step_size[None, :] * direction
        residual = residual - step_size[None, :] * image
        norm_next = lax.optimization_barrier(jnp.sum(residual * residual, axis=0))
        direction = residual + (norm_next / norm_now)[None, :] * direction
        norm_now = norm_next
    return merged
```

```python
import functools

import jax
import jax.numpy as jnp
from jax import lax
from jax.experimental import pallas as pl
from jax.experimental.pallas import tpu as pltpu
from jax.sharding import PartitionSpec as P

MESH = pl.DeviceIdType.MESH
F32, BF16 = jnp.float32, jnp.bfloat16
WIDTH = 5120
EPSILON = 1e-06
MIXING = 0.9
ITERS = 4
MODELS = 8
QUART = 640
LANES = 2 * QUART
CHUNK = 256
COLS = 16


def dot(a, b):
    return jnp.dot(a, b, preferred_element_type=F32)


def dot_nt(a, b):
    return lax.dot_general(a, b, (((1,), (1,)), ((), ())), preferred_element_type=F32)


def place():
    t = lax.axis_index("tok")
    x = lax.axis_index("row")
    c = lax.axis_index("col")
    return t, x, c


class Copies:
    def __init__(self, send, recv):
        self.send, self.recv, self.n = send, recv, 0

    def start(self, src, dst, device):
        copy = pltpu.make_async_remote_copy(
            src_ref=src,
            dst_ref=dst,
            send_sem=self.send.at[self.n],
            recv_sem=self.recv.at[self.n],
            device_id=device,
            device_id_type=MESH,
        )
        self.n += 1
        copy.start()
        return copy


def prepare_kernel(h_ref, g_ref, len_ref, out_ref, sums, halves, pieces, sq_send, sq_recv, send, recv):
    t, x, c = place()
    core, zl = lax.rem(t, 2), lax.div(t, 2)
    me = x * 8 + c

    def block(k):
        other = lax.rem(me + k, 32)
        return {"row": lax.div(other, 8), "col": lax.rem(other, 8)}

    def line(k):
        return {"tok": lax.rem(zl + k, 4) * 2 + core}

    sibling = {"tok": zl * 2 + 1 - core}
    barrier = pltpu.get_barrier_semaphore()

    def greet(k, _):
        pl.semaphore_signal(barrier, inc=1, device_id=block(k), device_id_type=MESH)
        return 0

    lax.fori_loop(1, 32, greet, 0)
    for k in range(1, 4):
        pl.semaphore_signal(barrier, inc=1, device_id=line(k), device_id_type=MESH)
    pl.semaphore_signal(barrier, inc=1, device_id=sibling, device_id_type=MESH)

    h = h_ref[...].astype(F32)
    squares = jnp.sum(h * h, axis=0, keepdims=True)
    sums[me] = jnp.zeros((8, 128), F32)
    for k in range(4):
        sums[me, k : k + 1, :] = squares[:, 128 * k : 128 * k + 128]
    pl.semaphore_wait(barrier, 35)

    def sums_copy(k):
        return pltpu.make_async_remote_copy(
            src_ref=sums.at[me],
            dst_ref=sums.at[me],
            send_sem=sq_send.at[k],
            recv_sem=sq_recv.at[k],
            device_id=block(k),
            device_id_type=MESH,
        )

    def send_sums(k, _):
        sums_copy(k).start()
        return 0

    def wait_sums(k, _):
        sums_copy(k).wait()
        return 0

    lax.fori_loop(1, 32, send_sums, 0)
    lax.fori_loop(1, 32, wait_sums, 0)
    total = jnp.sum(sums[...], axis=0)
    inverse = lax.rsqrt(total / WIDTH + EPSILON)
    inverse = jnp.concatenate([inverse[k : k + 1] for k in range(4)], axis=1)
    slot = lax.broadcasted_iota(jnp.int32, (1, 512), 1)
    live = (slot < len_ref[t]).astype(F32)
    normed = (h * (inverse * live) * g_ref[...]).astype(BF16)
    halves[0] = normed[:80]
    halves[1] = normed[80:]

    copies = Copies(send, recv)
    mine = lax.div(zl, 2)
    moved = []
    for k in range(1, 4):
        target = lax.rem(zl + k, 4)
        moved.append(copies.start(halves.at[lax.div(target, 2)], pieces.at[t], line(k)))
    pieces[t] = halves[mine]
    handed = [copies.start(pieces.at[t], pieces.at[t], sibling)]
    for k in range(1, 4):
        moved[k - 1].wait_recv()
        model = lax.rem(zl + 4 - k, 4) * 2 + core
        handed.append(copies.start(pieces.at[model], pieces.at[model], sibling))
    for copy in handed:
        copy.wait_recv()

    window = lax.rem(t, 4) * QUART
    source = lax.broadcasted_iota(jnp.int32, (512, QUART), 0)
    shift = source - lax.broadcasted_iota(jnp.int32, (512, QUART), 1)

    def add_model(m, carry):
        acc, first = carry
        size = len_ref[m]
        pick = jnp.where((shift == window - first) & (source < size), 1.0, 0.0).astype(BF16)
        return acc + dot(pieces[m], pick), first + size

    acc, _ = lax.fori_loop(0, MODELS, add_model, (jnp.zeros((80, QUART), F32), jnp.int32(0)))
    out_ref[...] = acc.astype(BF16).reshape(5, 16, QUART)
    for copy in moved + handed:
        copy.wait_send()


def prepare(hidden_t, gains_t, lengths):
    return pl.pallas_call(
        prepare_kernel,
        out_shape=jax.ShapeDtypeStruct((5, 16, QUART), BF16),
        in_specs=[
            pl.BlockSpec(memory_space=pltpu.VMEM),
            pl.BlockSpec(memory_space=pltpu.VMEM),
            pl.BlockSpec(memory_space=pltpu.SMEM),
        ],
        out_specs=pl.BlockSpec(memory_space=pltpu.VMEM),
        scratch_shapes=[
            pltpu.VMEM((32, 8, 128), F32),
            pltpu.VMEM((2, 80, 512), BF16),
            pltpu.VMEM((MODELS, 80, 512), BF16),
            pltpu.SemaphoreType.DMA((32,)),
            pltpu.SemaphoreType.DMA((32,)),
            pltpu.SemaphoreType.DMA((7,)),
            pltpu.SemaphoreType.DMA((7,)),
        ],
        compiler_params=pltpu.CompilerParams(
            collective_id=0, has_side_effects=True, vmem_limit_bytes=32 * 2**20
        ),
    )(hidden_t, gains_t, lengths)


def gather(n_ref, copies, t, x, c, later):
    core = lax.rem(t, 2)
    y, z = lax.rem(c, 4), lax.div(c, 4) * 4 + lax.div(t, 2)

    def at_x(k):
        return {"row": lax.rem(x + k + 4, 4)}

    def at_y(k):
        return {"col": lax.div(c, 4) * 4 + lax.rem(y + k + 4, 4)}

    def at_z(k):
        zz = lax.rem(z + k + 8, 8)
        return {"tok": lax.rem(zz, 4) * 2 + core, "col": lax.div(zz, 4) * 4 + y}

    def zpos(k):
        zz = lax.rem(z + k + 8, 8)
        lanes = pl.ds(pl.multiple_of(lax.rem(zz, 2) * QUART, 128), QUART)
        return lax.div(zz, 4), lax.rem(lax.div(zz, 2), 2), lanes

    def go(ref, device):
        return copies.start(ref, ref, device)

    zh, half, lanes = zpos(0)
    every = slice(None)
    rows_a, rows_b, rows_c = pl.ds(0, 1), pl.ds(1, 2), pl.ds(3, 2)

    own_b = n_ref.at[x, zh, y, half, rows_b, every, lanes]
    own_c = n_ref.at[x, zh, y, half, rows_c, every, lanes]
    own_a = n_ref.at[x, zh, y, half, rows_a, every, lanes]
    b1 = [go(own_b, at_y(k)) for k in (1, -1, 2)]
    c1 = [go(own_c, at_z(k)) for k in (1, -1, 2, -2, 3, -3, 4)]
    a1 = [go(own_a, at_x(k)) for k in (1, -1, 2)]

    def b2(k, part):
        h, f, l = zpos(k)
        return n_ref.at[x, h, pl.ds(2 * part, 2), f, rows_b, every, l]

    def c2(k, part):
        return n_ref.at[lax.rem(x + k + 4, 4), part, y, every, rows_c, every, every]

    for copy in b1:
        copy.wait_recv()
    right = [[go(b2(0, p), at_z(1)) for p in (0, 1)]]
    left = [[go(b2(0, p), at_z(-1)) for p in (1, 0)][::-1]]
    for copy in c1:
        copy.wait_recv()
    c_right = [go(c2(0, p), at_x(1)) for p in (0, 1)]
    c_left = [go(c2(0, p), at_x(-1)) for p in (1, 0)][::-1]
    for copy in a1:
        copy.wait_recv()
    own_a = n_ref.at[every, zh, y, half, rows_a, every, lanes]
    a2 = [go(own_a, at_y(k)) for k in (1, -1, 2)]
    for step in (1, 2):
        r, l = [], []
        for p in (0, 1):
            right[step - 1][p].wait_recv()
            r.append(go(b2(-step, p), at_z(1)))
            left[step - 1][1 - p].wait_recv()
            l.append(go(b2(step, 1 - p), at_z(-1)))
        right.append(r)
        left.append(l[::-1])
        if step == 1:
            c_right[0].wait_recv()
            c_far = [go(c2(-1, 0), at_x(1))]
            c_left[1].wait_recv()
            c_far.append(go(c2(1, 1), at_x(-1)))
    right[2][0].wait_recv()
    b_far = [go(b2(-3, 0), at_z(1))]
    left[2][1].wait_recv()
    b_far.append(go(b2(3, 1), at_z(-1)))
    c_right[1].wait_recv()
    c_left[0].wait_recv()
    for copy in c_far:
        copy.wait_recv()

    def c3(k, part):
        return n_ref.at[every, part, lax.rem(y + k + 4, 4), every, rows_c, every, every]

    def b3(k, part):
        return n_ref.at[lax.rem(x + k + 4, 4), part, every, every, rows_b, every, every]

    def a3(k, part):
        h, f, l = zpos(k)
        return n_ref.at[pl.ds(2 * part, 2), h, every, f, rows_a, every, l]

    c3_right = [go(c3(0, p), at_y(1)) for p in (0, 1)]
    c3_left = [go(c3(0, p), at_y(-1)) for p in (1, 0)][::-1]
    right[2][1].wait_recv()
    left[2][0].wait_recv()
    for copy in b_far:
        copy.wait_recv()
    b3_right = [go(b3(0, p), at_x(1)) for p in (0, 1)]
    b3_left = [go(b3(0, p), at_x(-1)) for p in (1, 0)][::-1]
    for copy in a2:
        copy.wait_recv()
    a_right = [[go(a3(0, p), at_z(1)) for p in (0, 1)]]
    a_left = [[go(a3(0, p), at_z(-1)) for p in (1, 0)][::-1]]
    far = []

    def a_step(step):
        r, l = [], []
        for p in (0, 1):
            a_right[step - 1][p].wait_recv()
            r.append(go(a3(-step, p), at_z(1)))
            a_left[step - 1][1 - p].wait_recv()
            l.append(go(a3(step, 1 - p), at_z(-1)))
        a_right.append(r)
        a_left.append(l[::-1])

    later()
    a_step(1)
    c3_right[0].wait_recv()
    far.append(go(c3(-1, 0), at_y(1)))
    c3_left[1].wait_recv()
    far.append(go(c3(1, 1), at_y(-1)))
    b3_right[0].wait_recv()
    far.append(go(b3(-1, 0), at_x(1)))
    b3_left[1].wait_recv()
    far.append(go(b3(1, 1), at_x(-1)))
    a_step(2)
    a_right[2][0].wait_recv()
    far.append(go(a3(-3, 0), at_z(1)))
    a_left[2][1].wait_recv()
    far.append(go(a3(3, 1), at_z(-1)))
    for copy in (a_right[2][1], a_left[2][0], c3_right[1], c3_left[0], b3_right[1], b3_left[0]):
        copy.wait_recv()
    for copy in far:
        copy.wait_recv()
    sent = b1 + c1 + a1 + a2 + c_right + c_left + c_far + b_far + c3_right + c3_left
    sent += b3_right + b3_left + far
    for pairs in (right, left, a_right, a_left):
        for pair in pairs:
            sent += pair
    return sent


def split(v):
    high = v.astype(BF16)
    low = (v - high.astype(F32)).astype(BF16)
    return jnp.concatenate([high, low], axis=0)


def fold(v):
    return v[:COLS] + v[COLS:]


def solve_kernel(
    piece_ref, w_ref, len_ref, out_ref,
    n_ref, wbuf, d2, image, sq, other, other_sq, norm, other_norm, direction, residual, merged, blocks, landed,
    send, recv,
):
    t, x, c = place()
    core, zl = lax.rem(t, 2), lax.div(t, 2)
    zh, y = lax.div(c, 4), lax.rem(c, 4)
    chip = x * 4 + zl
    sibling = {"tok": zl * 2 + 1 - core}

    def plane(k):
        target = lax.rem(chip + k, 16)
        return {"row": lax.div(target, 4), "tok": lax.rem(target, 4) * 2 + core}

    barrier = pltpu.get_barrier_semaphore()

    def greet(k, _):
        pl.semaphore_signal(barrier, inc=1, device_id=plane(k), device_id_type=MESH)
        return 0

    lax.fori_loop(1, 16, greet, 0)
    for k in (1, 2, 3):
        pl.semaphore_signal(
            barrier, inc=1, device_id={"col": zh * 4 + lax.rem(y + k, 4)}, device_id_type=MESH
        )
    for k in range(4):
        pl.semaphore_signal(
            barrier, inc=1, device_id={"tok": k * 2 + core, "col": (1 - zh) * 4 + y}, device_id_type=MESH
        )
    pl.semaphore_signal(barrier, inc=1, device_id=sibling, device_id_type=MESH)

    lanes = pl.ds(pl.multiple_of(lax.rem(zl, 2) * QUART, 128), QUART)
    n_ref[x, zh, y, lax.div(zl, 2), :, :, lanes] = piece_ref[...]
    pl.semaphore_wait(barrier, 23)

    copies = Copies(send, recv)

    def w_lanes(k):
        return pl.ds(pl.multiple_of(lax.rem(lax.div(chip + 16 - k, 4), 4) * 1280, 128), 1280)

    def w_slot(k):
        return wbuf.at[lax.rem(chip + 16 - k, 4) * 2 + core, :, w_lanes(k)]

    w_moved = []
    for k in range(1, 16):
        w_moved.append(copies.start(w_ref.at[lax.rem(chip + k, 16)], w_slot(0), plane(k)))
    wbuf[t, :, w_lanes(0)] = w_ref[chip]
    w_handed = [copies.start(w_slot(0), w_slot(0), sibling)]

    def hand_weights():
        for k in range(1, 16):
            w_moved[k - 1].wait_recv()
            w_handed.append(copies.start(w_slot(k), w_slot(k), sibling))

    sent = gather(n_ref, copies, t, x, c, hand_weights)
    for copy in w_handed:
        copy.wait_recv()

    def block_of(xx, offset):
        return n_ref[xx, :, :, :, :, :, pl.ds(offset, CHUNK)].reshape(1280, CHUNK)

    def features(xx):
        return slice(xx * 1280, xx * 1280 + 1280)

    image[...] = jnp.zeros_like(image)
    sq[...] = jnp.zeros_like(sq)

    def right_chunk(step, _):
        offset = pl.multiple_of(step * CHUNK, CHUNK)
        lane = lax.broadcasted_iota(jnp.int32, (1, CHUNK), 1) + offset
        slot = lane + core * QUART + jnp.where(lane >= QUART, QUART, 0)
        product = jnp.zeros((MODELS * COLS, CHUNK), F32)
        for xx in range(4):
            weights = wbuf[:, :, features(xx)].reshape(MODELS * COLS, 1280)
            product = product + dot(weights, block_of(xx, offset))
        outputs = jnp.zeros((COLS, CHUNK), F32)
        first = jnp.int32(0)
        masks = []
        for m in range(MODELS):
            size = len_ref[m]
            mask = jnp.where((slot >= first) & (slot < first + size), 1.0, 0.0)
            first = first + size
            masks.append(mask)
            outputs = outputs + mask * product[COLS * m : COLS * m + COLS]
        outputs = outputs.astype(BF16)
        masks = jnp.concatenate(masks, axis=0).astype(BF16)
        for xx in range(4):
            block = block_of(xx, offset)
            image[:, features(xx)] += dot_nt(outputs, block)
            sq[:, features(xx)] += dot_nt(masks, block * block)
        return 0

    lax.fori_loop(0, LANES // CHUNK, right_chunk, 0)
    swap = [
        copies.start(image, other.at[0], sibling),
        copies.start(sq, other_sq, sibling),
    ]
    swap[0].wait_recv()
    swap[1].wait_recv()
    squared = sq[...] + other_sq[...]
    right = MIXING * (image[...] + other[0])
    for m in range(MODELS):
        right = right + (1.0 - MIXING) * squared[m : m + 1] * wbuf[m].astype(F32)
    diagonal = (1.0 - MIXING) * jnp.sum(squared, axis=0, keepdims=True)
    direction[...] = right
    residual[...] = right
    norm_now = jnp.sum(right * right, axis=1, keepdims=True)
    swap[0].wait_send()
    swap[1].wait_send()

    def project(offset):
        total = jnp.zeros((2 * COLS, CHUNK), F32)
        for xx in range(4):
            total = total + dot(d2[:, features(xx)], block_of(xx, offset))
        return fold(total)

    def image_chunk(step, _):
        offset = pl.multiple_of(step * CHUNK, CHUNK)
        both = split(project(offset))
        for xx in range(4):
            image[:, features(xx)] += fold(dot_nt(both, block_of(xx, offset)))
        return 0

    def norm_chunk(step, total):
        part = project(pl.multiple_of(step * CHUNK, CHUNK))
        part = part * part
        return total + part[:, :128] + part[:, 128:]

    for step in range(ITERS):
        d2[...] = split(direction[...])
        if step < ITERS - 1:
            image[...] = jnp.zeros_like(image)
            lax.fori_loop(0, LANES // CHUNK, image_chunk, 0)
            swap = copies.start(image, other.at[step + 1], sibling)
            swap.wait_recv()
            now = direction[...]
            full = MIXING * (image[...] + other[step + 1]) + diagonal * now
            curvature = jnp.sum(now * full, axis=1, keepdims=True)
            step_size = norm_now / curvature
            rest = residual[...] - step_size * full
            residual[...] = rest
            norm_next = jnp.sum(rest * rest, axis=1, keepdims=True)
            if step == 0:
                merged[...] = step_size * now
            else:
                merged[...] += step_size * now
            direction[...] = rest + (norm_next / norm_now) * now
            norm_now = norm_next
            swap.wait_send()
        else:
            norm[...] = lax.fori_loop(0, LANES // CHUNK, norm_chunk, jnp.zeros((COLS, 128), F32))
            swap = copies.start(norm, other_norm, sibling)
            swap.wait_recv()
            now = direction[...]
            inner = jnp.sum(norm[...] + other_norm[...], axis=1, keepdims=True)
            curvature = MIXING * inner + jnp.sum(diagonal * now * now, axis=1, keepdims=True)
            result = merged[...] + (norm_now / curvature) * now
            swap.wait_send()

    blocks[...] = jnp.zeros_like(blocks)
    for b in range(32):
        blocks[b, :, 0:160] = result[:, 160 * b : 160 * b + 160]
    landed[chip] = blocks[x * 8 + t]
    moved = []
    for k in range(1, 16):
        target = lax.rem(chip + k, 16)
        target = lax.div(target, 4) * 8 + lax.rem(target, 4) * 2 + core
        moved.append(copies.start(blocks.at[target], landed.at[chip], plane(k)))
    for copy in moved:
        copy.wait_recv()
    out_ref[...] = landed[...].reshape(256, 256)
    for copy in sent + w_moved + w_handed + moved:
        copy.wait_send()


def solve(piece, weights_t, lengths):
    vmem = pl.BlockSpec(memory_space=pltpu.VMEM)
    wide = (COLS, WIDTH)
    count = 160
    return pl.pallas_call(
        solve_kernel,
        out_shape=jax.ShapeDtypeStruct((256, 256), F32),
        in_specs=[vmem, vmem, pl.BlockSpec(memory_space=pltpu.SMEM)],
        out_specs=vmem,
        scratch_shapes=[
            pltpu.VMEM((4, 2, 4, 2, 5, 16, LANES), BF16),
            pltpu.VMEM((MODELS, COLS, WIDTH), BF16),
            pltpu.VMEM((2 * COLS, WIDTH), BF16),
            pltpu.VMEM(wide, F32),
            pltpu.VMEM((MODELS, WIDTH), F32),
            pltpu.VMEM((ITERS, COLS, WIDTH), F32),
            pltpu.VMEM((MODELS, WIDTH), F32),
            pltpu.VMEM((COLS, 128), F32),
            pltpu.VMEM((COLS, 128), F32),
            pltpu.VMEM(wide, F32),
            pltpu.VMEM(wide, F32),
            pltpu.VMEM(wide, F32),
            pltpu.VMEM((32, COLS, 256), F32),
            pltpu.VMEM((16, COLS, 256), F32),
            pltpu.SemaphoreType.DMA((count,)),
            pltpu.SemaphoreType.DMA((count,)),
        ],
        compiler_params=pltpu.CompilerParams(
            collective_id=1, has_side_effects=True, vmem_limit_bytes=56 * 2**20
        ),
    )(piece, weights_t, lengths)


def body(hidden, gains, weights, lengths):
    piece = prepare(hidden.T, gains.T, lengths)
    merged = solve(piece, weights[0].T.reshape(16, COLS, 1280), lengths)
    return merged[:, :160].T


def solution(mesh):
    return jax.shard_map(
        body,
        mesh=mesh,
        in_specs=(P("tok", ("row", "col")), P("tok", ("row", "col")), P("tok", "row", "col"), P()),
        out_specs=P(("row", "tok"), "col"),
        check_vma=False,
    )
```

```python
import functools

import jax
import jax.numpy as jnp
from jax import lax
from jax.experimental import pallas as pl
from jax.experimental.pallas import tpu as pltpu
from jax.sharding import PartitionSpec as P

MESH = pl.DeviceIdType.MESH
F32, BF16 = jnp.float32, jnp.bfloat16
WIDTH = 5120
EPSILON = 1e-06
MIXING = 0.9
ITERS = 4
MODELS = 8
QUART = 640
LANES = 2 * QUART
CHUNK = 256
COLS = 16


def dot(a, b):
    return jnp.dot(a, b, preferred_element_type=F32)


def dot_nt(a, b):
    return lax.dot_general(a, b, (((1,), (1,)), ((), ())), preferred_element_type=F32)


def place():
    t = lax.axis_index("tok")
    x = lax.axis_index("row")
    c = lax.axis_index("col")
    return t, x, c


class Copies:
    def __init__(self, send, recv):
        self.send, self.recv, self.n = send, recv, 0

    def start(self, src, dst, device):
        copy = pltpu.make_async_remote_copy(
            src_ref=src,
            dst_ref=dst,
            send_sem=self.send.at[self.n],
            recv_sem=self.recv.at[self.n],
            device_id=device,
            device_id_type=MESH,
        )
        self.n += 1
        copy.start()
        return copy


class Plan:
    RATE, HOP = 45e3, 2.3

    def __init__(self):
        self.tasks = []

    def add(self, ref, device, link, size, deps, hops=1):
        self.tasks.append((ref, device, link, size, tuple(deps), hops))
        return len(self.tasks) - 1

    def ring(self, ref, device, axis, n, size, deps, way):
        deps = list(deps)
        right = [self.add(ref(0), device(1), axis + "+", size, deps)]
        left = [self.add(ref(0), device(-1), axis + "-", size, deps)]
        for k in range(1, n // 2 - 1):
            right.append(self.add(ref(-k), device(1), axis + "+", size, right[-1:]))
            left.append(self.add(ref(k), device(-1), axis + "-", size, left[-1:]))
        last = n // 2 - 1
        if way == 0:
            far = self.add(ref(-last), device(1), axis + "+", size, right[-1:])
        else:
            far = self.add(ref(last), device(-1), axis + "-", size, left[-1:])
        arrived = {0: deps, n // 2: [far]}
        for k in range(1, n // 2):
            arrived[-k] = [right[k - 1]]
            arrived[k] = [left[k - 1]]
        return arrived

    def straight(self, ref, device, axis, n, size, deps):
        arrived = {0: list(deps)}
        for k in sorted(range(1 - n // 2, n // 2 + 1), key=abs):
            if k:
                link = axis + ("-" if k < 0 else "+")
                one = self.add(ref(0), device(k), link, size * abs(k), deps, abs(k))
                arrived[k if k == n // 2 else -k] = [one]
        return arrived

    def order(self):
        free, arrival, placed = {}, {}, []
        while len(placed) < len(self.tasks):
            best = None
            for i, (_, _, link, size, deps, hops) in enumerate(self.tasks):
                if i in arrival or any(d not in arrival for d in deps):
                    continue
                ready = max([arrival[d] for d in deps], default=0.0)
                key = (ready, i)
                if best is None or key < best[0]:
                    best = (key, i)
            (ready, _), i = best
            _, _, link, size, _, hops = self.tasks[i]
            begin = max(ready, free.get(link, 0.0))
            free[link] = begin + size / self.RATE
            arrival[i] = free[link] + self.HOP + 0.7 * (hops - 1)
            placed.append(i)
        return placed, arrival

    def run(self, copies, extra=()):
        placed, arrival = self.order()
        extra = sorted(extra, key=lambda e: e[0])
        started, waited = {}, set()

        def wait(i):
            if i not in waited:
                waited.add(i)
                started[i].wait_recv()

        for i in placed:
            ref, device, _, _, deps, _ = self.tasks[i]
            ready = max([arrival[d] for d in deps], default=0.0)
            while extra and extra[0][0] <= ready:
                extra.pop(0)[1]()
            for d in deps:
                wait(d)
            started[i] = copies.start(ref, ref, device)
        for _, call in extra:
            call()
        for i in sorted(arrival, key=arrival.get):
            wait(i)
        return [started[i] for i in placed]


def gather_plan(n_ref, t, x, c):
    core = lax.rem(t, 2)
    y, z = lax.rem(c, 4), lax.div(c, 4) * 4 + lax.div(t, 2)
    every = slice(None)
    plan = Plan()
    unit = 16 * 128 * 2

    def xx(k):
        return lax.rem(x + k + 4, 4)

    def yy(k):
        return lax.rem(y + k + 4, 4)

    def at_x(k):
        return {"row": xx(k)}

    def at_y(k):
        return {"col": lax.div(c, 4) * 4 + yy(k)}

    def at_z(k):
        zz = lax.rem(z + k + 8, 8)
        return {"tok": lax.rem(zz, 4) * 2 + core, "col": lax.div(zz, 4) * 4 + y}

    def zpos(k, first, tiles):
        zz = lax.rem(z + k + 8, 8)
        start = lax.rem(zz, 2) * QUART + first * 128
        lanes = pl.ds(pl.multiple_of(start, 128), tiles * 128)
        return lax.div(zz, 4), lax.rem(lax.div(zz, 2), 2), lanes

    rows_ab, rows_c = pl.ds(0, 3), pl.ds(3, 2)
    size_a, size_b, size_c = 6 * unit, 9 * unit, 10 * unit

    def part_a(kx, ky, kz):
        h, f, l = zpos(kz, 0, 2)
        return n_ref.at[every if kx is None else xx(kx), h, every if ky is None else yy(ky), f, rows_ab, every, l]

    def part_b(kx, ky, kz):
        h, f, l = zpos(kz, 2, 3)
        return n_ref.at[every if kx is None else xx(kx), h, every if ky is None else yy(ky), f, rows_ab, every, l]

    def part_c(kx, ky, kz):
        if kz is None:
            return n_ref.at[xx(kx), every, yy(ky), every, rows_c, every, every]
        h, f, l = zpos(kz, 0, 5)
        return n_ref.at[every if kx is None else xx(kx), h, yy(ky), f, rows_c, every, l]

    def all_of(arrived):
        return [i for ids in arrived.values() for i in ids]

    b1 = plan.straight(lambda k: part_b(0, k, 0), at_y, "y", 4, size_b, [])
    c1 = plan.straight(lambda k: part_c(0, 0, k), at_z, "z", 8, size_c, [])
    a1 = plan.straight(lambda k: part_a(k, 0, 0), at_x, "x", 4, size_a, [])
    b2 = plan.ring(lambda k: part_b(0, None, k), at_z, "z", 8, 4 * size_b, all_of(b1), 0)
    a2 = plan.straight(lambda k: part_a(None, k, 0), at_y, "y", 4, 4 * size_a, all_of(a1))
    c2 = {0: all_of(c1), 1: [], -1: [], 2: []}
    for way, k in enumerate((0, 1, -1, 2, -2, 3, -3, 4)):
        got = plan.ring(lambda kx, k=k: part_c(kx, 0, k), at_x, "x", 4, size_c, c1[k], way % 2)
        for kx in (1, -1, 2):
            c2[kx] += got[kx]
    for way, k in enumerate((0, 1, -1, 2)):
        plan.ring(lambda ky, k=k: part_c(k, ky, None), at_y, "y", 4, 8 * size_c, c2[k], way % 2)
    for way, k in enumerate((0, 1, -1, 2, -2, 3, -3, 4)):
        plan.ring(lambda kx, k=k: part_b(kx, None, k), at_x, "x", 4, 4 * size_b, b2[k], way % 2)
    for way, k in enumerate((0, 1, -1, 2)):
        plan.ring(lambda kz, k=k: part_a(None, k, kz), at_z, "z", 8, 4 * size_a, a2[k], way % 2)
    return plan


def split(v):
    high = v.astype(BF16)
    low = (v - high.astype(F32)).astype(BF16)
    return jnp.concatenate([high, low], axis=0)


def fold(v):
    return v[:COLS] + v[COLS:]


def row_of(tile):
    return jnp.concatenate([tile[k : k + 1] for k in range(4)], axis=1)


def solve_kernel(
    h_ref, g_ref, w_ref, len_ref, out_ref,
    sums, scales, halves, pieces, wt, n_ref, wbuf, d2, image, sq, other, other_sq, norm, other_norm, direction, residual,
    merged, blocks, landed, sq_send, sq_recv, send, recv,
):
    t, x, c = place()
    core, zl = lax.rem(t, 2), lax.div(t, 2)
    zh, y = lax.div(c, 4), lax.rem(c, 4)
    chip, me = x * 4 + zl, x * 8 + c
    sibling = {"tok": zl * 2 + 1 - core}

    def plane(k):
        target = lax.rem(chip + k, 16)
        return {"row": lax.div(target, 4), "tok": lax.rem(target, 4) * 2 + core}

    def block(k):
        target = lax.rem(me + k, 32)
        return {"row": lax.div(target, 8), "col": lax.rem(target, 8)}

    def line(k, side):
        return {"tok": lax.rem(zl + k, 4) * 2 + side}

    barrier = pltpu.get_barrier_semaphore()

    def greet(device):
        pl.semaphore_signal(barrier, inc=1, device_id=device, device_id_type=MESH)

    def greet_block(k, _):
        greet(block(k))
        return 0

    lax.fori_loop(1, 32, greet_block, 0)
    for k in range(1, 4):
        zz = lax.rem(zl + k, 4)
        greet(line(k, core))
        greet(line(k, 1 - core))
        greet({"tok": zz * 2 + core, "col": (1 - zh) * 4 + y})
        for kx in range(1, 4):
            greet({"row": lax.rem(x + kx, 4), "tok": zz * 2 + core})
    greet(sibling)

    h = h_ref[...].astype(F32)
    squares = jnp.sum(h * h, axis=0, keepdims=True)
    sums[me] = jnp.zeros((8, 128), F32)
    for k in range(4):
        sums[me, k : k + 1, :] = squares[:, 128 * k : 128 * k + 128]
    halves[0] = h_ref[:80]
    halves[1] = h_ref[80:]
    scales[t] = jnp.zeros((8, 128), F32)
    scales[t, 4:5, 0:80] = g_ref[:, 0:80]
    scales[t, 5:6, 0:80] = g_ref[:, 80:160]
    mine = lax.div(zl, 2)
    pieces[t] = halves[mine]
    pl.semaphore_wait(barrier, 50)

    def sums_copy(k):
        return pltpu.make_async_remote_copy(
            src_ref=sums.at[me],
            dst_ref=sums.at[me],
            send_sem=sq_send.at[k],
            recv_sem=sq_recv.at[k],
            device_id=block(k),
            device_id_type=MESH,
        )

    def send_sums(k, _):
        sums_copy(k).start()
        return 0

    def wait_sums(k, _):
        sums_copy(k).wait()
        return 0

    lax.fori_loop(1, 32, send_sums, 0)

    copies = Copies(send, recv)
    moved = []
    for k in range(1, 4):
        target = lax.rem(zl + k, 4)
        moved.append(copies.start(halves.at[lax.div(target, 2)], pieces.at[t], line(k, core)))
    handed = [copies.start(pieces.at[t], pieces.at[t], sibling)]

    eye = lax.broadcasted_iota(jnp.int32, (256, 256), 0) == lax.broadcasted_iota(jnp.int32, (256, 256), 1)
    eye = jnp.where(eye, 1.0, 0.0).astype(BF16)
    wt[...] = dot_nt(eye, w_ref[...]).astype(BF16).reshape(16, COLS, 1280)

    def w_lanes(k):
        return pl.ds(pl.multiple_of(lax.rem(lax.div(chip + 16 - k, 4), 4) * 1280, 128), 1280)

    def w_slot(k):
        return wbuf.at[lax.rem(chip + 16 - k, 4) * 2 + core, :, w_lanes(k)]

    wbuf[t, :, w_lanes(0)] = wt[chip]
    w_moved, w_handed = [], []

    def send_weights():
        for k in range(1, 16):
            w_moved.append(copies.start(wt.at[lax.rem(chip + k, 16)], w_slot(0), plane(k)))
        w_handed.append(copies.start(w_slot(0), w_slot(0), sibling))

    def hand_weights():
        for k in range(1, 16):
            w_moved[k - 1].wait_recv()
            w_handed.append(copies.start(w_slot(k), w_slot(k), sibling))

    lax.fori_loop(1, 32, wait_sums, 0)
    inverse = lax.rsqrt(jnp.sum(sums[...], axis=0) / WIDTH + EPSILON)
    slot = lax.broadcasted_iota(jnp.int32, (8, 128), 0) * 128 + lax.broadcasted_iota(jnp.int32, (8, 128), 1)
    live = (slot < len_ref[t]).astype(F32)
    scales[t, 0:4, :] = (inverse * live)[0:4]
    scaled = [copies.start(scales.at[t], scales.at[t], sibling)]
    for k in range(1, 4):
        scaled.append(copies.start(scales.at[t], scales.at[t], line(k, core)))
        scaled.append(copies.start(scales.at[t], scales.at[t], line(k, 1 - core)))
    for k in range(1, 4):
        moved[k - 1].wait_recv()
        model = lax.rem(zl + 4 - k, 4) * 2 + core
        handed.append(copies.start(pieces.at[model], pieces.at[model], sibling))
    send_weights()
    for copy in scaled + handed:
        copy.wait_recv()

    window = lax.rem(t, 4) * QUART
    source = lax.broadcasted_iota(jnp.int32, (512, QUART), 0)
    shift = source - lax.broadcasted_iota(jnp.int32, (512, QUART), 1)
    spread = lax.broadcasted_iota(jnp.int32, (80, 128), 0) == lax.broadcasted_iota(jnp.int32, (80, 128), 1)

    def add_model(m, carry):
        acc, first = carry
        size = len_ref[m]
        scale = scales[m]
        gain = jnp.where(mine == 0, scale[4:5], scale[5:6])
        gain = jnp.sum(jnp.where(spread, gain, 0.0), axis=1, keepdims=True)
        normed = (pieces[m].astype(F32) * row_of(scale) * gain).astype(BF16)
        pick = jnp.where((shift == window - first) & (source < size), 1.0, 0.0).astype(BF16)
        return acc + dot(normed, pick), first + size

    acc, _ = lax.fori_loop(0, MODELS, add_model, (jnp.zeros((80, QUART), F32), jnp.int32(0)))
    lanes = pl.ds(pl.multiple_of(lax.rem(zl, 2) * QUART, 128), QUART)
    n_ref[x, zh, y, mine, :, :, lanes] = acc.astype(BF16).reshape(5, 16, QUART)

    sent = gather_plan(n_ref, t, x, c).run(copies, [(8.0, hand_weights)])
    for copy in w_handed:
        copy.wait_recv()
    sent += moved + handed + scaled

    def block_of(xx):
        return n_ref[xx].reshape(1280, LANES)

    def features(xx):
        return slice(xx * 1280, xx * 1280 + 1280)

    def swap_image(xx, slot):
        part = features(xx)
        return copies.start(image.at[:, part], other.at[slot, :, part], sibling)

    def right_chunk(step, _):
        offset = pl.multiple_of(step * CHUNK, CHUNK)
        lane = lax.broadcasted_iota(jnp.int32, (1, CHUNK), 1) + offset
        slot = lane + core * QUART + jnp.where(lane >= QUART, QUART, 0)
        product = jnp.zeros((MODELS * COLS, CHUNK), F32)
        for xx in range(4):
            weights = wbuf[:, :, features(xx)].reshape(MODELS * COLS, 1280)
            block = n_ref[xx, :, :, :, :, :, pl.ds(offset, CHUNK)].reshape(1280, CHUNK)
            product = product + dot(weights, block)
        outputs = jnp.zeros((COLS, CHUNK), F32)
        first = jnp.int32(0)
        masks = []
        for m in range(MODELS):
            size = len_ref[m]
            mask = jnp.where((slot >= first) & (slot < first + size), 1.0, 0.0)
            first = first + size
            masks.append(mask)
            outputs = outputs + mask * product[COLS * m : COLS * m + COLS]
        masks = jnp.concatenate(masks + masks, axis=0)
        d2[:, pl.ds(offset, CHUNK)] = jnp.concatenate([outputs, masks], axis=0).astype(BF16)
        return 0

    lax.fori_loop(0, LANES // CHUNK, right_chunk, 0)
    swaps = []
    for xx in range(4):
        block = block_of(xx)
        image[:, features(xx)] = dot_nt(d2[:COLS, :LANES], block)
        swaps.append(swap_image(xx, 0))
        sq[:, features(xx)] = dot_nt(d2[COLS:, :LANES], block * block)[:MODELS]
        swaps.append(copies.start(sq.at[:, features(xx)], other_sq.at[:, features(xx)], sibling))
    for copy in swaps:
        copy.wait_recv()
    squared = sq[...] + other_sq[...]
    right = MIXING * (image[...] + other[0])
    for m in range(MODELS):
        right = right + (1.0 - MIXING) * squared[m : m + 1] * wbuf[m].astype(F32)
    diagonal = (1.0 - MIXING) * jnp.sum(squared, axis=0, keepdims=True)
    direction[...] = right
    residual[...] = right
    norm_now = jnp.sum(right * right, axis=1, keepdims=True)
    for copy in swaps:
        copy.wait_send()

    def project():
        total = jnp.zeros((2 * COLS, LANES), F32)
        for xx in range(4):
            total = total + dot(d2[:, features(xx)], block_of(xx))
        return fold(total)

    for step in range(ITERS):
        d2[...] = split(direction[...])
        if step < ITERS - 1:
            both = split(project())
            swaps = []
            for xx in range(4):
                image[:, features(xx)] = fold(dot_nt(both, block_of(xx)))
                swaps.append(swap_image(xx, step + 1))
            for copy in swaps:
                copy.wait_recv()
            now = direction[...]
            full = MIXING * (image[...] + other[step + 1]) + diagonal * now
            curvature = jnp.sum(now * full, axis=1, keepdims=True)
            step_size = norm_now / curvature
            rest = residual[...] - step_size * full
            residual[...] = rest
            norm_next = jnp.sum(rest * rest, axis=1, keepdims=True)
            if step == 0:
                merged[...] = step_size * now
            else:
                merged[...] += step_size * now
            direction[...] = rest + (norm_next / norm_now) * now
            norm_now = norm_next
            for copy in swaps:
                copy.wait_send()
        else:
            inner = project()
            inner = jnp.sum(inner * inner, axis=1, keepdims=True)
            norm[...] = jnp.broadcast_to(inner, (COLS, 128))
            swap = copies.start(norm, other_norm, sibling)
            swap.wait_recv()
            now = direction[...]
            inner = (norm[...] + other_norm[...])[:, :1]
            curvature = MIXING * inner + jnp.sum(diagonal * now * now, axis=1, keepdims=True)
            result = merged[...] + (norm_now / curvature) * now
            swap.wait_send()

    blocks[...] = jnp.zeros_like(blocks)
    for b in range(32):
        blocks[b, :, 0:160] = result[:, 160 * b : 160 * b + 160]
    landed[chip] = blocks[x * 8 + t]
    moved = []
    for k in range(1, 16):
        target = lax.rem(chip + k, 16)
        target = lax.div(target, 4) * 8 + lax.rem(target, 4) * 2 + core
        moved.append(copies.start(blocks.at[target], landed.at[chip], plane(k)))
    for copy in moved:
        copy.wait_recv()
    out_ref[...] = landed[...].reshape(256, 256)
    for copy in sent + w_moved + w_handed + moved:
        copy.wait_send()


def body(hidden, gains, weights, lengths):
    vmem = pl.BlockSpec(memory_space=pltpu.VMEM)
    wide = (COLS, WIDTH)
    count = 200
    merged = pl.pallas_call(
        solve_kernel,
        out_shape=jax.ShapeDtypeStruct((256, 256), F32),
        in_specs=[vmem, vmem, vmem, pl.BlockSpec(memory_space=pltpu.SMEM)],
        out_specs=vmem,
        scratch_shapes=[
            pltpu.VMEM((32, 8, 128), F32),
            pltpu.VMEM((MODELS, 8, 128), F32),
            pltpu.VMEM((2, 80, 512), BF16),
            pltpu.VMEM((MODELS, 80, 512), BF16),
            pltpu.VMEM((16, COLS, 1280), BF16),
            pltpu.VMEM((4, 2, 4, 2, 5, 16, LANES), BF16),
            pltpu.VMEM((MODELS, COLS, WIDTH), BF16),
            pltpu.VMEM((2 * COLS, WIDTH), BF16),
            pltpu.VMEM(wide, F32),
            pltpu.VMEM((MODELS, WIDTH), F32),
            pltpu.VMEM((ITERS, COLS, WIDTH), F32),
            pltpu.VMEM((MODELS, WIDTH), F32),
            pltpu.VMEM((COLS, 128), F32),
            pltpu.VMEM((COLS, 128), F32),
            pltpu.VMEM(wide, F32),
            pltpu.VMEM(wide, F32),
            pltpu.VMEM(wide, F32),
            pltpu.VMEM((32, COLS, 256), F32),
            pltpu.VMEM((16, COLS, 256), F32),
            pltpu.SemaphoreType.DMA((32,)),
            pltpu.SemaphoreType.DMA((32,)),
            pltpu.SemaphoreType.DMA((count,)),
            pltpu.SemaphoreType.DMA((count,)),
        ],
        compiler_params=pltpu.CompilerParams(
            collective_id=0, has_side_effects=True, vmem_limit_bytes=56 * 2**20
        ),
    )(hidden.T, gains, weights[0], lengths)
    return merged[:, :160].T


def solution(mesh):
    return jax.shard_map(
        body,
        mesh=mesh,
        in_specs=(P("tok", ("row", "col")), P("tok", ("row", "col")), P("tok", "row", "col"), P()),
        out_specs=P(("row", "tok"), "col"),
        check_vma=False,
    )
```

```python
import functools

import jax
import jax.numpy as jnp
from jax import lax
from jax.experimental import pallas as pl
from jax.experimental.pallas import tpu as pltpu
from jax.sharding import PartitionSpec as P

MESH = pl.DeviceIdType.MESH
F32, BF16 = jnp.float32, jnp.bfloat16
WIDTH = 5120
EPSILON = 1e-06
MIXING = 0.9
ITERS = 4
MODELS = 8
QUART = 640
LANES = 2 * QUART
LIVE = 2304
CHUNK = 256
COLS = 16


def dot(a, b):
    return jnp.dot(a, b, preferred_element_type=F32)


def dot_nt(a, b):
    return lax.dot_general(a, b, (((1,), (1,)), ((), ())), preferred_element_type=F32)


def place():
    t = lax.axis_index("tok")
    x = lax.axis_index("row")
    c = lax.axis_index("col")
    return t, x, c


class Copies:
    def __init__(self, send, recv):
        self.send, self.recv, self.n = send, recv, 0

    def start(self, src, dst, device):
        copy = pltpu.make_async_remote_copy(
            src_ref=src,
            dst_ref=dst,
            send_sem=self.send.at[self.n],
            recv_sem=self.recv.at[self.n],
            device_id=device,
            device_id_type=MESH,
        )
        self.n += 1
        copy.start()
        return copy


class Plan:
    RATE, HOP = 45e3, 2.3

    def __init__(self):
        self.tasks = []

    def add(self, ref, device, link, size, deps, hops=1):
        self.tasks.append((ref, device, link, size, tuple(deps), hops))
        return len(self.tasks) - 1

    def ring(self, ref, device, axis, n, size, deps, way):
        deps = list(deps)
        right = [self.add(ref(0), device(1), axis + "+", size, deps)]
        left = [self.add(ref(0), device(-1), axis + "-", size, deps)]
        for k in range(1, n // 2 - 1):
            right.append(self.add(ref(-k), device(1), axis + "+", size, right[-1:]))
            left.append(self.add(ref(k), device(-1), axis + "-", size, left[-1:]))
        last = n // 2 - 1
        if way == 0:
            far = self.add(ref(-last), device(1), axis + "+", size, right[-1:])
        else:
            far = self.add(ref(last), device(-1), axis + "-", size, left[-1:])
        arrived = {0: deps, n // 2: [far]}
        for k in range(1, n // 2):
            arrived[-k] = [right[k - 1]]
            arrived[k] = [left[k - 1]]
        return arrived

    def straight(self, ref, device, axis, n, size, deps):
        arrived = {0: list(deps)}
        for k in sorted(range(1 - n // 2, n // 2 + 1), key=abs):
            if k:
                link = axis + ("-" if k < 0 else "+")
                one = self.add(ref(0), device(k), link, size * abs(k), deps, abs(k))
                arrived[k if k == n // 2 else -k] = [one]
        return arrived

    def order(self):
        count = len(self.tasks)
        rank = [0.0] * count
        for i in reversed(range(count)):
            _, _, _, size, deps, hops = self.tasks[i]
            rank[i] += size / self.RATE + self.HOP + 0.7 * (hops - 1)
            for d in deps:
                rank[d] = max(rank[d], rank[i])
        free, arrival, placed, begins = {}, {}, [], {}
        while len(placed) < count:
            ready = {}
            for i, (_, _, link, _, deps, _) in enumerate(self.tasks):
                if i not in arrival and all(d in arrival for d in deps):
                    ready[i] = max([arrival[d] for d in deps] + [free.get(link, 0.0)])
            first = min(ready, key=lambda i: (round(ready[i], 3), -rank[i], i))
            _, _, link, size, _, hops = self.tasks[first]
            begins[first] = ready[first]
            free[link] = ready[first] + size / self.RATE
            arrival[first] = free[link] + self.HOP + 0.7 * (hops - 1)
            placed.append(first)
        return placed, arrival, begins

    def run(self, copies, extra=()):
        placed, arrival, begins = self.order()
        extra = sorted(extra, key=lambda e: e[0])
        started, waited = {}, set()

        def wait(i):
            if i not in waited:
                waited.add(i)
                started[i].wait_recv()

        for i in placed:
            ref, device, _, _, deps, _ = self.tasks[i]
            while extra and extra[0][0] <= begins[i]:
                extra.pop(0)[1]()
            for d in deps:
                wait(d)
            started[i] = copies.start(ref, ref, device)
        for _, call in extra:
            call()
        for i in sorted(arrival, key=arrival.get):
            wait(i)
        return [started[i] for i in placed]


def gather_plan(n_ref, t, x, c):
    core = lax.rem(t, 2)
    y, z = lax.rem(c, 4), lax.div(c, 4) * 4 + lax.div(t, 2)
    every = slice(None)
    plan = Plan()
    unit = 16 * 128 * 2

    def xx(k):
        return lax.rem(x + k + 4, 4)

    def yy(k):
        return lax.rem(y + k + 4, 4)

    def at_x(k):
        return {"row": xx(k)}

    def at_y(k):
        return {"col": lax.div(c, 4) * 4 + yy(k)}

    def at_z(k):
        zz = lax.rem(z + k + 8, 8)
        return {"tok": lax.rem(zz, 4) * 2 + core, "col": lax.div(zz, 4) * 4 + y}

    def zpos(k, first, tiles):
        zz = lax.rem(z + k + 8, 8)
        start = lax.rem(zz, 2) * QUART + first * 128
        lanes = pl.ds(pl.multiple_of(start, 128), tiles * 128)
        return lax.div(zz, 4), lax.rem(lax.div(zz, 2), 2), lanes

    rows_ab, rows_c = pl.ds(0, 3), pl.ds(3, 2)
    size_a, size_b, size_c = 6 * unit, 9 * unit, 10 * unit

    def part_a(kx, ky, kz):
        h, f, l = zpos(kz, 0, 2)
        return n_ref.at[every if kx is None else xx(kx), h, every if ky is None else yy(ky), f, rows_ab, every, l]

    def part_b(kx, ky, kz):
        h, f, l = zpos(kz, 2, 3)
        return n_ref.at[every if kx is None else xx(kx), h, every if ky is None else yy(ky), f, rows_ab, every, l]

    def part_c(kx, ky, kz):
        if kz is None:
            return n_ref.at[xx(kx), every, yy(ky), every, rows_c, every, every]
        h, f, l = zpos(kz, 0, 5)
        return n_ref.at[every if kx is None else xx(kx), h, yy(ky), f, rows_c, every, l]

    def all_of(arrived):
        return [i for ids in arrived.values() for i in ids]

    b1 = plan.straight(lambda k: part_b(0, k, 0), at_y, "y", 4, size_b, [])
    c1 = plan.ring(lambda k: part_c(0, 0, k), at_z, "z", 8, size_c, [], 1)
    a1 = plan.straight(lambda k: part_a(k, 0, 0), at_x, "x", 4, size_a, [])
    b2 = plan.ring(lambda k: part_b(0, None, k), at_z, "z", 8, 4 * size_b, all_of(b1), 0)
    a2 = plan.ring(lambda k: part_a(None, k, 0), at_y, "y", 4, 4 * size_a, all_of(a1), 1)
    c2 = {0: all_of(c1), 1: [], -1: [], 2: []}
    c2z = {}
    for way, k in enumerate((0, 1, -1, 2, -2, 3, -3, 4)):
        got = plan.ring(lambda kx, k=k: part_c(kx, 0, k), at_x, "x", 4, size_c, c1[k], way % 2)
        for kx in (1, -1, 2):
            c2[kx] += got[kx]
        c2z[k] = got
    for way, k in enumerate((0, 1, -1, 2)):
        for kz in (0, 1, -1, 2, -2, 3, -3, 4):
            plan.ring(lambda ky, k=k, kz=kz: part_c(k, ky, kz), at_y, "y", 4, size_c, c2z[kz][k], (way + kz) % 2)
    for way, k in enumerate((0, 1, -1, 2, -2, 3, -3, 4)):
        plan.ring(lambda kx, k=k: part_b(kx, None, k), at_x, "x", 4, 4 * size_b, b2[k], way % 2)
    for way, k in enumerate((0, 1, -1, 2)):
        plan.ring(lambda kz, k=k: part_a(None, k, kz), at_z, "z", 8, 4 * size_a, a2[k], way % 2)
    return plan


def split(v):
    high = v.astype(BF16)
    low = (v - high.astype(F32)).astype(BF16)
    return jnp.concatenate([high, low], axis=0)


def fold(v):
    return v[:COLS] + v[COLS:]


def row_of(tile):
    return jnp.concatenate([tile[k : k + 1] for k in range(4)], axis=1)


def solve_kernel(
    h_ref, g_ref, w_ref, len_ref, out_ref,
    sums, scales, halves, pieces, wt, n_ref, wbuf, d2, image, sq, other, other_sq, norm, other_norm, direction, residual,
    merged, diagonal, squared_norm, size, ub, blocks, landed, last_blocks, last_landed, sq_send, sq_recv,
    swap_send, swap_recv, norm_send, norm_recv, out_send, out_recv, send, recv,
):
    t, x, c = place()
    core, zl = lax.rem(t, 2), lax.div(t, 2)
    zh, y = lax.div(c, 4), lax.rem(c, 4)
    chip, me = x * 4 + zl, x * 8 + c
    sibling = {"tok": zl * 2 + 1 - core}

    def plane(k):
        target = lax.rem(chip + k, 16)
        return {"row": lax.div(target, 4), "tok": lax.rem(target, 4) * 2 + core}

    def block(k):
        target = lax.rem(me + k, 32)
        return {"row": lax.div(target, 8), "col": lax.rem(target, 8)}

    def line(k, side):
        return {"tok": lax.rem(zl + k, 4) * 2 + side}

    barrier = pltpu.get_barrier_semaphore()

    def greet(device):
        pl.semaphore_signal(barrier, inc=1, device_id=device, device_id_type=MESH)

    def greet_block(k, _):
        greet(block(k))
        return 0

    lax.fori_loop(1, 32, greet_block, 0)
    for k in range(1, 4):
        zz = lax.rem(zl + k, 4)
        greet(line(k, core))
        greet(line(k, 1 - core))
        greet({"tok": zz * 2 + core, "col": (1 - zh) * 4 + y})
        for kx in range(1, 4):
            greet({"row": lax.rem(x + kx, 4), "tok": zz * 2 + core})
    greet(sibling)

    h = h_ref[...].astype(F32)
    squares = jnp.sum(h * h, axis=0, keepdims=True)
    sums[me] = jnp.zeros((8, 128), F32)
    for k in range(4):
        sums[me, k : k + 1, :] = squares[:, 128 * k : 128 * k + 128]
    halves[0] = h_ref[:80]
    halves[1] = h_ref[80:]
    scales[t] = jnp.zeros((8, 128), F32)
    scales[t, 4:5, 0:80] = g_ref[:, 0:80]
    scales[t, 5:6, 0:80] = g_ref[:, 80:160]
    mine = lax.div(zl, 2)
    pieces[t] = halves[mine]
    blocks[...] = jnp.zeros_like(blocks)
    last_blocks[...] = jnp.zeros_like(last_blocks)
    pl.semaphore_wait(barrier, 50)

    def sums_copy(k):
        return pltpu.make_async_remote_copy(
            src_ref=sums.at[me],
            dst_ref=sums.at[me],
            send_sem=sq_send.at[k],
            recv_sem=sq_recv.at[k],
            device_id=block(k),
            device_id_type=MESH,
        )

    def send_sums(k, _):
        sums_copy(k).start()
        return 0

    def wait_sums(k, _):
        sums_copy(k).wait()
        return 0

    lax.fori_loop(1, 32, send_sums, 0)

    copies = Copies(send, recv)
    moved = []
    for k in range(1, 4):
        target = lax.rem(zl + k, 4)
        moved.append(copies.start(halves.at[lax.div(target, 2)], pieces.at[t], line(k, core)))
    handed = [copies.start(pieces.at[t], pieces.at[t], sibling)]

    eye = lax.broadcasted_iota(jnp.int32, (256, 256), 0) == lax.broadcasted_iota(jnp.int32, (256, 256), 1)
    eye = jnp.where(eye, 1.0, 0.0).astype(BF16)
    wt[...] = dot_nt(eye, w_ref[...]).astype(BF16).reshape(16, COLS, 1280)

    def w_lanes(k):
        return pl.ds(pl.multiple_of(lax.rem(lax.div(chip + 16 - k, 4), 4) * 1280, 128), 1280)

    def w_slot(k):
        return wbuf.at[lax.rem(chip + 16 - k, 4) * 2 + core, :, w_lanes(k)]

    wbuf[t, :, w_lanes(0)] = wt[chip]
    w_moved, w_handed = [], []

    def send_weights():
        for k in range(1, 16):
            w_moved.append(copies.start(wt.at[lax.rem(chip + k, 16)], w_slot(0), plane(k)))
        w_handed.append(copies.start(w_slot(0), w_slot(0), sibling))

    def hand_weights():
        for k in range(1, 16):
            w_moved[k - 1].wait_recv()
            w_handed.append(copies.start(w_slot(k), w_slot(k), sibling))

    lax.fori_loop(1, 32, wait_sums, 0)
    inverse = lax.rsqrt(jnp.sum(sums[...], axis=0) / WIDTH + EPSILON)
    slot = lax.broadcasted_iota(jnp.int32, (8, 128), 0) * 128 + lax.broadcasted_iota(jnp.int32, (8, 128), 1)
    live = (slot < len_ref[t]).astype(F32)
    scales[t, 0:4, :] = (inverse * live)[0:4]
    scaled = [copies.start(scales.at[t], scales.at[t], sibling)]
    for k in range(1, 4):
        scaled.append(copies.start(scales.at[t], scales.at[t], line(k, core)))
        scaled.append(copies.start(scales.at[t], scales.at[t], line(k, 1 - core)))
    for k in range(1, 4):
        moved[k - 1].wait_recv()
        model = lax.rem(zl + 4 - k, 4) * 2 + core
        handed.append(copies.start(pieces.at[model], pieces.at[model], sibling))
    send_weights()
    for copy in scaled + handed:
        copy.wait_recv()

    window = lax.rem(t, 4) * QUART
    shift = lax.broadcasted_iota(jnp.int32, (512, QUART), 0)
    shift = shift - lax.broadcasted_iota(jnp.int32, (512, QUART), 1)
    spread = lax.broadcasted_iota(jnp.int32, (80, 128), 0) == lax.broadcasted_iota(jnp.int32, (80, 128), 1)

    lane = lax.broadcasted_iota(jnp.int32, (80, 128), 1)

    def add_model(m, carry):
        acc, tile, first = carry
        size = len_ref[m]
        scale = scales[m]
        gain = jnp.where(mine == 0, scale[4:5], scale[5:6])
        gain = jnp.sum(jnp.where(spread, gain, 0.0), axis=1, keepdims=True)
        normed = (pieces[m].astype(F32) * row_of(scale) * gain).astype(BF16)
        pick = jnp.where(shift == window - first, 1.0, 0.0).astype(BF16)
        wide_normed = normed.astype(F32)
        total = jnp.sum(wide_normed * wide_normed, axis=1, keepdims=True)
        tile = jnp.where(lax.rem(lane, 8) == m, total, tile)
        return acc + dot(normed, pick), tile, first + size

    zero = (jnp.zeros((80, QUART), F32), jnp.zeros((80, 128), F32), jnp.int32(0))
    acc, tile, _ = lax.fori_loop(0, MODELS, add_model, zero)
    high = tile.astype(BF16).astype(F32)
    middle = (tile - high).astype(BF16).astype(F32)
    tile = jnp.where(lane < 8, high, jnp.where(lane < 16, middle, tile - high - middle))
    tile = jnp.where(lane < 24, tile, 0.0)
    acc = jnp.concatenate([acc[:, :512], acc[:, 512:] + jnp.where(lax.rem(t, 4) == 3, tile, 0.0)], axis=1)
    lanes = pl.ds(pl.multiple_of(lax.rem(zl, 2) * QUART, 128), QUART)
    n_ref[x, zh, y, mine, :, :, lanes] = acc.astype(BF16).reshape(5, 16, QUART)

    sent = gather_plan(n_ref, t, x, c).run(copies, [(8.0, hand_weights)])
    for copy in w_handed:
        copy.wait_recv()
    sent += moved + handed + scaled

    def block_of(xx):
        return n_ref[xx].reshape(1280, LANES)

    def features(xx):
        return pl.ds(pl.multiple_of(xx * 1280, 128), 1280)

    def each(body, init=0):
        return lax.fori_loop(0, 4, body, init)

    def fold_lanes(v):
        return functools.reduce(jnp.add, [v[:, 128 * k : 128 * k + 128] for k in range(10)])

    def swap_copy(slot, xx):
        return pltpu.make_async_remote_copy(
            src_ref=image.at[:, features(xx)],
            dst_ref=other.at[slot, :, features(xx)],
            send_sem=swap_send.at[slot * 4 + xx],
            recv_sem=swap_recv.at[slot * 4 + xx],
            device_id=sibling,
            device_id_type=MESH,
        )

    def norm_copy(step):
        return pltpu.make_async_remote_copy(
            src_ref=norm.at[step],
            dst_ref=other_norm.at[step],
            send_sem=norm_send.at[step],
            recv_sem=norm_recv.at[step],
            device_id=sibling,
            device_id_type=MESH,
        )

    def slots(first, count):
        at = lax.broadcasted_iota(jnp.int32, (1, count), 1) + first
        return at + core * QUART + jnp.where(at >= QUART, QUART, 0)

    take = lax.broadcasted_iota(jnp.int32, (16, 128), 1)
    take = (lax.rem(take, 8) == lax.broadcasted_iota(jnp.int32, (16, 128), 0)) & (take < 24)
    take = jnp.where(take, 1.0, 0.0).astype(BF16)

    def squares_part(xx, _):
        spare = n_ref[xx, :, :, :, :, :, LANES - 128 :].reshape(1280, 128)
        sq[:, features(xx)] = dot_nt(take, spare)[:MODELS]
        return 0

    each(squares_part)
    swap_sq = copies.start(sq, other_sq, sibling)

    def right_chunk(step, _):
        offset = pl.multiple_of(step * CHUNK, CHUNK)
        slot = slots(offset, CHUNK)
        product = jnp.zeros((MODELS * COLS, CHUNK), F32)
        for xx in range(4):
            weights = wbuf[:, :, xx * 1280 : xx * 1280 + 1280].reshape(MODELS * COLS, 1280)
            block = n_ref[xx, :, :, :, :, :, pl.ds(offset, CHUNK)].reshape(1280, CHUNK)
            product = product + dot(weights, block)
        outputs = jnp.zeros((COLS, CHUNK), F32)
        first = jnp.int32(0)
        for m in range(MODELS):
            size = len_ref[m]
            mask = jnp.where((slot >= first) & (slot < first + size), 1.0, 0.0)
            first = first + size
            outputs = outputs + mask * product[COLS * m : COLS * m + COLS]
        ub[:COLS, pl.ds(offset, CHUNK)] = outputs.astype(BF16)
        return 0

    def right_part(xx, total):
        swap_copy(0, xx).wait_recv()
        part = features(xx)
        right = MIXING * (image[:, part] + other[0, :, part])
        squared = jnp.where(core == 1, sq[:, part], other_sq[:, part])
        for m in range(MODELS):
            right = right + (1.0 - MIXING) * squared[m : m + 1] * wbuf[m, :, part].astype(F32)
        diagonal[0:1, part] = (1.0 - MIXING) * jnp.sum(squared, axis=0, keepdims=True)
        direction[:, part] = right
        residual[:, part] = right
        d2[:, part] = split(right)
        return total + fold_lanes(right * right)

    def spread_out(v):
        return jnp.broadcast_to(jnp.sum(v, axis=1, keepdims=True), (COLS, 128))

    def block_copy(k, source, target, first):
        to = lax.rem(chip + k, 16)
        to = lax.div(to, 4) * 8 + lax.rem(to, 4) * 2 + core
        return pltpu.make_async_remote_copy(
            src_ref=source.at[to],
            dst_ref=target.at[chip],
            send_sem=out_send.at[first + k],
            recv_sem=out_recv.at[first + k],
            device_id=plane(k),
            device_id_type=MESH,
        )

    def send_blocks(values, source, target, first):
        def cut(group, _):
            value = values(pl.ds(pl.multiple_of(group * 640, 128), 640))
            for k in range(4):
                source[group * 4 + k, :, 0:160] = value[:, 160 * k : 160 * k + 160].astype(source.dtype)
            return 0

        def send_one(k, _):
            block_copy(k, source, target, first).start()
            return 0

        lax.fori_loop(0, 8, cut, 0)
        target[chip] = source[x * 8 + t]
        lax.fori_loop(1, 16, send_one, 0)

    def solve_step(step, _):
        @pl.when(step == 0)
        def _():
            lax.fori_loop(0, LANES // CHUNK, right_chunk, 0)
            ub[COLS:] = jnp.zeros((COLS, LANES), BF16)

        @pl.when(step > 0)
        def _():
            total = jnp.zeros((2 * COLS, LANES), F32)
            for xx in range(4):
                total = total + dot(d2[:, 1280 * xx : 1280 * xx + 1280], block_of(xx))
            projected = fold(total) * jnp.where(slots(0, LANES) < LIVE, 1.0, 0.0)
            norm[step] = spread_out(fold_lanes(projected * projected))
            norm_copy(step).start()
            ub[...] = split(projected)

        @pl.when(step < ITERS)
        def _():
            def back_part(xx, _):
                image[:, features(xx)] = fold(dot_nt(ub[...], block_of(xx)))
                swap_copy(step, xx).start()
                return 0

            each(back_part)

        @pl.when(step == 0)
        def _():
            swap_sq.wait()
            squared_norm[...] = spread_out(each(right_part, jnp.zeros((COLS, 128), F32)))
            merged[...] = jnp.zeros_like(merged)

        @pl.when(step > 0)
        def _():
            def weighted(xx, total):
                now = direction[:, features(xx)]
                return total + fold_lanes(diagonal[0:1, features(xx)] * now * now)

            inner = spread_out(each(weighted, jnp.zeros((COLS, 128), F32)))
            norm_copy(step).wait()
            curvature = MIXING * (norm[step] + other_norm[step]) + inner
            size[...] = squared_norm[...] / curvature

        @pl.when((step > 0) & (step < ITERS))
        def _():
            factor = size[:, :1]
            merged[...] += factor * direction[...]

            @pl.when(step == ITERS - 1)
            def _():
                send_blocks(lambda part: merged[:, part], blocks, landed, 0)

            def residual_part(xx, total):
                part = features(xx)
                swap_copy(step, xx).wait_recv()
                full = MIXING * (image[:, part] + other[step, :, part]) + diagonal[0:1, part] * direction[:, part]
                rest = residual[:, part] - factor * full
                residual[:, part] = rest
                return total + fold_lanes(rest * rest)

            norm_next = spread_out(each(residual_part, jnp.zeros((COLS, 128), F32)))
            ratio = (norm_next / squared_norm[...])[:, :1]
            squared_norm[...] = norm_next

            def direction_part(xx, _):
                part = features(xx)
                now = residual[:, part] + ratio * direction[:, part]
                direction[:, part] = now
                d2[:, part] = split(now)
                return 0

            each(direction_part)

        @pl.when(step < ITERS)
        def _():
            def sent_part(xx, _):
                swap_copy(step, xx).wait_send()
                return 0

            each(sent_part)

        return 0

    lax.fori_loop(0, ITERS + 1, solve_step, 0)
    send_blocks(lambda part: size[:, :1] * direction[:, part], last_blocks, last_landed, 16)

    def wait_blocks(k, _):
        block_copy(k, blocks, landed, 0).wait()
        block_copy(k, last_blocks, last_landed, 16).wait()
        return 0

    lax.fori_loop(1, 16, wait_blocks, 0)
    result = landed[...] + last_landed[...].astype(F32)
    out_ref[...] = result.reshape(256, 256).T[:160]
    for copy in sent + w_moved + w_handed:
        copy.wait_send()


def body(hidden, gains, weights, lengths):
    vmem = pl.BlockSpec(memory_space=pltpu.VMEM)
    wide = (COLS, WIDTH)
    count = 250
    return pl.pallas_call(
        solve_kernel,
        out_shape=jax.ShapeDtypeStruct((160, 256), F32),
        in_specs=[vmem, vmem, vmem, pl.BlockSpec(memory_space=pltpu.SMEM)],
        out_specs=vmem,
        scratch_shapes=[
            pltpu.VMEM((32, 8, 128), F32),
            pltpu.VMEM((MODELS, 8, 128), F32),
            pltpu.VMEM((2, 80, 512), BF16),
            pltpu.VMEM((MODELS, 80, 512), BF16),
            pltpu.VMEM((16, COLS, 1280), BF16),
            pltpu.VMEM((4, 2, 4, 2, 5, 16, LANES), BF16),
            pltpu.VMEM((MODELS, COLS, WIDTH), BF16),
            pltpu.VMEM((2 * COLS, WIDTH), BF16),
            pltpu.VMEM(wide, F32),
            pltpu.VMEM((MODELS, WIDTH), F32),
            pltpu.VMEM((ITERS, COLS, WIDTH), F32),
            pltpu.VMEM((MODELS, WIDTH), F32),
            pltpu.VMEM((ITERS + 1, COLS, 128), F32),
            pltpu.VMEM((ITERS + 1, COLS, 128), F32),
            pltpu.VMEM(wide, F32),
            pltpu.VMEM(wide, F32),
            pltpu.VMEM(wide, F32),
            pltpu.VMEM((8, WIDTH), F32),
            pltpu.VMEM((COLS, 128), F32),
            pltpu.VMEM((COLS, 128), F32),
            pltpu.VMEM((2 * COLS, LANES), BF16),
            pltpu.VMEM((32, COLS, 256), F32),
            pltpu.VMEM((16, COLS, 256), F32),
            pltpu.VMEM((32, COLS, 256), BF16),
            pltpu.VMEM((16, COLS, 256), BF16),
            pltpu.SemaphoreType.DMA((32,)),
            pltpu.SemaphoreType.DMA((32,)),
            pltpu.SemaphoreType.DMA((4 * ITERS,)),
            pltpu.SemaphoreType.DMA((4 * ITERS,)),
            pltpu.SemaphoreType.DMA((ITERS + 1,)),
            pltpu.SemaphoreType.DMA((ITERS + 1,)),
            pltpu.SemaphoreType.DMA((32,)),
            pltpu.SemaphoreType.DMA((32,)),
            pltpu.SemaphoreType.DMA((count,)),
            pltpu.SemaphoreType.DMA((count,)),
        ],
        compiler_params=pltpu.CompilerParams(
            collective_id=0, has_side_effects=True, vmem_limit_bytes=56 * 2**20
        ),
    )(hidden.T, gains, weights[0], lengths)


def solution(mesh):
    return jax.shard_map(
        body,
        mesh=mesh,
        in_specs=(P("tok", ("row", "col")), P("tok", ("row", "col")), P("tok", "row", "col"), P()),
        out_specs=P(("row", "tok"), "col"),
        check_vma=False,
    )
```

```python
import functools

import jax
import jax.numpy as jnp
from jax import lax
from jax.experimental import pallas as pl
from jax.experimental.pallas import tpu as pltpu
from jax.sharding import PartitionSpec as P

MESH = pl.DeviceIdType.MESH
F32, BF16 = jnp.float32, jnp.bfloat16
WIDTH = 5120
EPSILON = 1e-06
MIXING = 0.9
ITERS = 4
MODELS = 8
QUART = 640
LANES = 2 * QUART
LIVE = 2304
CHUNK = 256
COLS = 16


def dot(a, b):
    return jnp.dot(a, b, preferred_element_type=F32)


def dot_nt(a, b):
    return lax.dot_general(a, b, (((1,), (1,)), ((), ())), preferred_element_type=F32)


def place():
    t = lax.axis_index("tok")
    x = lax.axis_index("row")
    c = lax.axis_index("col")
    return t, x, c


class Copies:
    def __init__(self, send, recv):
        self.send, self.recv, self.n = send, recv, 0

    def start(self, src, dst, device):
        copy = pltpu.make_async_remote_copy(
            src_ref=src,
            dst_ref=dst,
            send_sem=self.send.at[self.n],
            recv_sem=self.recv.at[self.n],
            device_id=device,
            device_id_type=MESH,
        )
        self.n += 1
        copy.start()
        return copy


class Plan:
    RATE, HOP = 45e3, 2.3

    def __init__(self):
        self.tasks, self.level = [], []

    def add(self, ref, device, link, size, deps, hops=1, level=0):
        self.tasks.append((ref, device, link, size, tuple(deps), hops))
        self.level.append(level)
        return len(self.tasks) - 1

    def ring(self, ref, device, axis, n, size, deps, way, level=0, far_level=None):
        deps, far_level = list(deps), level if far_level is None else far_level
        right = [self.add(ref(0), device(1), axis + "+", size, deps, 1, level)]
        left = [self.add(ref(0), device(-1), axis + "-", size, deps, 1, level)]
        for k in range(1, n // 2 - 1):
            right.append(self.add(ref(-k), device(1), axis + "+", size, right[-1:], 1, level))
            left.append(self.add(ref(k), device(-1), axis + "-", size, left[-1:], 1, level))
        last = n // 2 - 1
        if way == 0:
            far = self.add(ref(-last), device(1), axis + "+", size, right[-1:], 1, far_level)
        else:
            far = self.add(ref(last), device(-1), axis + "-", size, left[-1:], 1, far_level)
        arrived = {0: deps, n // 2: [far]}
        for k in range(1, n // 2):
            arrived[-k] = [right[k - 1]]
            arrived[k] = [left[k - 1]]
        return arrived

    def straight(self, ref, device, axis, n, size, deps):
        arrived = {0: list(deps)}
        for k in sorted(range(1 - n // 2, n // 2 + 1), key=abs):
            if k:
                link = axis + ("-" if k < 0 else "+")
                one = self.add(ref(0), device(k), link, size * abs(k), deps, abs(k))
                arrived[k if k == n // 2 else -k] = [one]
        return arrived

    def order(self):
        count = len(self.tasks)
        rank = [0.0] * count
        for i in reversed(range(count)):
            _, _, _, size, deps, hops = self.tasks[i]
            rank[i] += size / self.RATE + self.HOP + 0.7 * (hops - 1)
            for d in deps:
                rank[d] = max(rank[d], rank[i])
        free, arrival, placed, begins = {}, {}, [], {}
        while len(placed) < count:
            ready = {}
            for i, (_, _, link, _, deps, _) in enumerate(self.tasks):
                if i not in arrival and all(d in arrival for d in deps):
                    ready[i] = max([arrival[d] for d in deps] + [free.get(link, 0.0)])
            first = min(ready, key=lambda i: (round(ready[i], 3), self.level[i], -rank[i], i))
            _, _, link, size, _, hops = self.tasks[first]
            begins[first] = ready[first]
            free[link] = ready[first] + size / self.RATE
            arrival[first] = free[link] + self.HOP + 0.7 * (hops - 1)
            placed.append(first)
        return placed, arrival, begins

    def run(self, copies, extra):
        placed, arrival, begins = self.order()
        extra = [(max([at] + [arrival[d] for d in deps]), deps, call) for at, deps, call in extra]
        extra = sorted(extra, key=lambda e: e[0])
        started, waited = {}, set()

        def wait(ids):
            for i in sorted(ids, key=arrival.get):
                if i not in waited:
                    waited.add(i)
                    started[i].wait_recv()

        def due(now):
            while extra and extra[0][0] + 0.5 <= now:
                _, deps, call = extra.pop(0)
                wait(deps)
                call()

        for i in placed:
            ref, device, _, _, deps, _ = self.tasks[i]
            due(begins[i])
            wait(deps)
            started[i] = copies.start(ref, ref, device)
        due(1e9)
        wait(arrival)
        return [started[i] for i in placed]


def gather_plan(n_ref, t, x, c):
    core = lax.rem(t, 2)
    y, z = lax.rem(c, 4), lax.div(c, 4) * 4 + lax.div(t, 2)
    every = slice(None)
    plan = Plan()
    unit = 16 * 128 * 2

    def xx(k):
        return lax.rem(x + k + 4, 4)

    def yy(k):
        return lax.rem(y + k + 4, 4)

    def at_x(k):
        return {"row": xx(k)}

    def at_y(k):
        return {"col": lax.div(c, 4) * 4 + yy(k)}

    def at_z(k):
        zz = lax.rem(z + k + 8, 8)
        return {"tok": lax.rem(zz, 4) * 2 + core, "col": lax.div(zz, 4) * 4 + y}

    def zpos(k, first, tiles):
        zz = lax.rem(z + k + 8, 8)
        start = lax.rem(zz, 2) * QUART + first * 128
        lanes = pl.ds(pl.multiple_of(start, 128), tiles * 128)
        return lax.div(zz, 4), lax.rem(lax.div(zz, 2), 2), lanes

    rows_ab, rows_c = pl.ds(0, 3), pl.ds(3, 2)
    size_a, size_b, size_c = 6 * unit, 9 * unit, 10 * unit

    def part_a(kx, ky, kz):
        h, f, l = zpos(kz, 0, 2)
        return n_ref.at[every if kx is None else xx(kx), h, every if ky is None else yy(ky), f, rows_ab, every, l]

    def part_b(kx, ky, kz):
        h, f, l = zpos(kz, 2, 3)
        return n_ref.at[every if kx is None else xx(kx), h, every if ky is None else yy(ky), f, rows_ab, every, l]

    def part_c(kx, ky, kz):
        if kz is None:
            return n_ref.at[xx(kx), every, yy(ky), every, rows_c, every, every]
        h, f, l = zpos(kz, 0, 5)
        return n_ref.at[every if kx is None else xx(kx), h, yy(ky), f, rows_c, every, l]

    def all_of(arrived):
        return [i for ids in arrived.values() for i in ids]

    b1 = plan.straight(lambda k: part_b(0, k, 0), at_y, "y", 4, size_b, [])
    c1 = plan.ring(lambda k: part_c(0, 0, k), at_z, "z", 8, size_c, [], 1)
    a1 = plan.straight(lambda k: part_a(k, 0, 0), at_x, "x", 4, size_a, [])
    b2 = plan.ring(lambda k: part_b(0, None, k), at_z, "z", 8, 4 * size_b, all_of(b1), 0)
    a2 = plan.ring(lambda k: part_a(None, k, 0), at_y, "y", 4, 4 * size_a, all_of(a1), 1)
    turns = ((0, 0), (1, 1), (-1, 1), (2, 2))
    whole = {0: all_of(b2), 1: [], -1: [], 2: []}
    c2 = {}
    for way, k in enumerate((0, 1, -1, 2, -2, 3, -3, 4)):
        c2[k] = plan.ring(lambda kx, k=k: part_c(kx, 0, k), at_x, "x", 4, size_c, c1[k], way % 2)
    for way, (k, level) in enumerate(turns):
        for kz in (0, 1, -1, 2, -2, 3, -3, 4):
            got = plan.ring(
                lambda ky, k=k, kz=kz: part_c(k, ky, kz), at_y, "y", 4, size_c, c2[kz][k], way % 2, level
            )
            whole[k] += all_of(got)
    for way, k in enumerate((0, 1, -1, 2, -2, 3, -3, 4)):
        got = plan.ring(
            lambda kx, k=k: part_b(kx, None, k), at_x, "x", 4, 4 * size_b, b2[k], way % 2, 1, 2
        )
        for kx in (1, -1, 2):
            whole[kx] += got[kx]
    for way, (k, level) in enumerate(turns):
        got = plan.ring(
            lambda kz, k=k: part_a(k, None, kz), at_z, "z", 8, 4 * size_a, all_of(a2), way % 2, level
        )
        whole[k] += all_of(got)
    return plan, whole


def split(v):
    high = v.astype(BF16)
    low = (v - high.astype(F32)).astype(BF16)
    return jnp.concatenate([high, low], axis=0)


def fold(v):
    return v[:COLS] + v[COLS:]


def row_of(tile):
    return jnp.concatenate([tile[k : k + 1] for k in range(4)], axis=1)


def solve_kernel(
    h_ref, g_ref, w_ref, len_ref, out_ref,
    sums, scales, halves, pieces, wt, n_ref, wbuf, d2, image, sq, other, other_sq, norm, other_norm, direction, residual,
    merged, diagonal, squared_norm, size, ub, product, turned, blocks, landed, last_blocks, last_landed, sq_send, sq_recv,
    swap_send, swap_recv, norm_send, norm_recv, out_send, out_recv, send, recv,
):
    t, x, c = place()
    core, zl = lax.rem(t, 2), lax.div(t, 2)
    zh, y = lax.div(c, 4), lax.rem(c, 4)
    chip, me = x * 4 + zl, x * 8 + c
    sibling = {"tok": zl * 2 + 1 - core}

    def plane(k):
        target = lax.rem(chip + k, 16)
        return {"row": lax.div(target, 4), "tok": lax.rem(target, 4) * 2 + core}

    def block(k):
        target = lax.rem(me + k, 32)
        return {"row": lax.div(target, 8), "col": lax.rem(target, 8)}

    def line(k, side):
        return {"tok": lax.rem(zl + k, 4) * 2 + side}

    barrier = pltpu.get_barrier_semaphore()

    def greet(device):
        pl.semaphore_signal(barrier, inc=1, device_id=device, device_id_type=MESH)

    def greet_block(k, _):
        greet(block(k))
        return 0

    lax.fori_loop(1, 32, greet_block, 0)
    for k in range(1, 4):
        zz = lax.rem(zl + k, 4)
        greet(line(k, core))
        greet(line(k, 1 - core))
        greet({"tok": zz * 2 + core, "col": (1 - zh) * 4 + y})
        for kx in range(1, 4):
            greet({"row": lax.rem(x + kx, 4), "tok": zz * 2 + core})
    greet(sibling)

    h = h_ref[...].astype(F32)
    squares = jnp.sum(h * h, axis=0, keepdims=True)
    sums[me] = jnp.zeros((8, 128), F32)
    for k in range(4):
        sums[me, k : k + 1, :] = squares[:, 128 * k : 128 * k + 128]
    halves[0] = h_ref[:80]
    halves[1] = h_ref[80:]
    scales[t] = jnp.zeros((8, 128), F32)
    scales[t, 4:5, 0:80] = g_ref[:, 0:80]
    scales[t, 5:6, 0:80] = g_ref[:, 80:160]
    mine = lax.div(zl, 2)
    pieces[t] = halves[mine]
    blocks[...] = jnp.zeros_like(blocks)
    last_blocks[...] = jnp.zeros_like(last_blocks)
    pl.semaphore_wait(barrier, 50)

    def sums_copy(k):
        return pltpu.make_async_remote_copy(
            src_ref=sums.at[me],
            dst_ref=sums.at[me],
            send_sem=sq_send.at[k],
            recv_sem=sq_recv.at[k],
            device_id=block(k),
            device_id_type=MESH,
        )

    def send_sums(k, _):
        sums_copy(k).start()
        return 0

    def wait_sums(k, _):
        sums_copy(k).wait()
        return 0

    lax.fori_loop(1, 32, send_sums, 0)

    copies = Copies(send, recv)
    moved = []
    for k in range(1, 4):
        target = lax.rem(zl + k, 4)
        moved.append(copies.start(halves.at[lax.div(target, 2)], pieces.at[t], line(k, core)))
    handed = [copies.start(pieces.at[t], pieces.at[t], sibling)]

    eye = lax.broadcasted_iota(jnp.int32, (256, 256), 0) == lax.broadcasted_iota(jnp.int32, (256, 256), 1)
    eye = jnp.where(eye, 1.0, 0.0).astype(BF16)
    wt[...] = dot_nt(eye, w_ref[...]).astype(BF16).reshape(16, COLS, 1280)

    def w_lanes(k):
        return pl.ds(pl.multiple_of(lax.rem(lax.div(chip + 16 - k, 4), 4) * 1280, 128), 1280)

    def w_slot(k):
        return wbuf.at[lax.rem(chip + 16 - k, 4) * 2 + core, :, w_lanes(k)]

    wbuf[t, :, w_lanes(0)] = wt[chip]
    w_moved, w_handed = [], []

    def send_weights():
        for k in range(1, 16):
            w_moved.append(copies.start(wt.at[lax.rem(chip + k, 16)], w_slot(0), plane(k)))
        w_handed.append(copies.start(w_slot(0), w_slot(0), sibling))

    def hand_weights():
        for k in range(1, 16):
            w_moved[k - 1].wait_recv()
            w_handed.append(copies.start(w_slot(k), w_slot(k), sibling))

    lax.fori_loop(1, 32, wait_sums, 0)
    inverse = lax.rsqrt(jnp.sum(sums[...], axis=0) / WIDTH + EPSILON)
    slot = lax.broadcasted_iota(jnp.int32, (8, 128), 0) * 128 + lax.broadcasted_iota(jnp.int32, (8, 128), 1)
    live = (slot < len_ref[t]).astype(F32)
    scales[t, 0:4, :] = (inverse * live)[0:4]
    scaled = [copies.start(scales.at[t], scales.at[t], sibling)]
    for k in range(1, 4):
        scaled.append(copies.start(scales.at[t], scales.at[t], line(k, core)))
        scaled.append(copies.start(scales.at[t], scales.at[t], line(k, 1 - core)))
    for k in range(1, 4):
        moved[k - 1].wait_recv()
        model = lax.rem(zl + 4 - k, 4) * 2 + core
        handed.append(copies.start(pieces.at[model], pieces.at[model], sibling))
    send_weights()
    for copy in scaled + handed:
        copy.wait_recv()

    window = lax.rem(t, 4) * QUART
    shift = lax.broadcasted_iota(jnp.int32, (512, QUART), 0)
    shift = shift - lax.broadcasted_iota(jnp.int32, (512, QUART), 1)
    spread = lax.broadcasted_iota(jnp.int32, (80, 128), 0) == lax.broadcasted_iota(jnp.int32, (80, 128), 1)

    lane = lax.broadcasted_iota(jnp.int32, (80, 128), 1)

    def add_model(m, carry):
        acc, tile, first = carry
        size = len_ref[m]
        scale = scales[m]
        gain = jnp.where(mine == 0, scale[4:5], scale[5:6])
        gain = jnp.sum(jnp.where(spread, gain, 0.0), axis=1, keepdims=True)
        normed = (pieces[m].astype(F32) * row_of(scale) * gain).astype(BF16)
        pick = jnp.where(shift == window - first, 1.0, 0.0).astype(BF16)
        wide_normed = normed.astype(F32)
        total = jnp.sum(wide_normed * wide_normed, axis=1, keepdims=True)
        tile = jnp.where(lax.rem(lane, 8) == m, total, tile)
        return acc + dot(normed, pick), tile, first + size

    zero = (jnp.zeros((80, QUART), F32), jnp.zeros((80, 128), F32), jnp.int32(0))
    acc, tile, _ = lax.fori_loop(0, MODELS, add_model, zero)
    high = tile.astype(BF16).astype(F32)
    middle = (tile - high).astype(BF16).astype(F32)
    tile = jnp.where(lane < 8, high, jnp.where(lane < 16, middle, tile - high - middle))
    tile = jnp.where(lane < 24, tile, 0.0)
    acc = jnp.concatenate([acc[:, :512], acc[:, 512:] + jnp.where(lax.rem(t, 4) == 3, tile, 0.0)], axis=1)
    lanes = pl.ds(pl.multiple_of(lax.rem(zl, 2) * QUART, 128), QUART)
    n_ref[x, zh, y, mine, :, :, lanes] = acc.astype(BF16).reshape(5, 16, QUART)

    def block_of(xx):
        return n_ref[xx].reshape(1280, LANES)

    def features(xx):
        return pl.ds(pl.multiple_of(xx * 1280, 128), 1280)

    def each(body, init=0):
        return lax.fori_loop(0, 4, body, init)

    def fold_lanes(v):
        return functools.reduce(jnp.add, [v[:, 128 * k : 128 * k + 128] for k in range(10)])

    def swap_copy(slot, xx):
        return pltpu.make_async_remote_copy(
            src_ref=image.at[:, features(xx)],
            dst_ref=other.at[slot, :, features(xx)],
            send_sem=swap_send.at[slot * 4 + xx],
            recv_sem=swap_recv.at[slot * 4 + xx],
            device_id=sibling,
            device_id_type=MESH,
        )

    def norm_copy(step):
        return pltpu.make_async_remote_copy(
            src_ref=norm.at[step],
            dst_ref=other_norm.at[step],
            send_sem=norm_send.at[step],
            recv_sem=norm_recv.at[step],
            device_id=sibling,
            device_id_type=MESH,
        )

    def slots(first, count):
        at = lax.broadcasted_iota(jnp.int32, (1, count), 1) + first
        return at + core * QUART + jnp.where(at >= QUART, QUART, 0)

    take = lax.broadcasted_iota(jnp.int32, (16, 128), 1)
    take = (lax.rem(take, 8) == lax.broadcasted_iota(jnp.int32, (16, 128), 0)) & (take < 24)
    take = jnp.where(take, 1.0, 0.0).astype(BF16)

    def use_block(k):
        xx = lax.rem(x + k + 4, 4)
        spare = n_ref[xx, :, :, :, :, :, LANES - 128 :].reshape(1280, 128)
        sq[:, features(xx)] = dot_nt(take, spare)[:MODELS]
        weights = wbuf[:, :, features(xx)].reshape(MODELS * COLS, 1280)

        def part(step, _):
            at = pl.ds(pl.multiple_of(step * CHUNK, CHUNK), CHUNK)
            block = n_ref[xx, :, :, :, :, :, at].reshape(1280, CHUNK)
            turned[xx, at, :] = block.T
            more = dot(weights, block)
            product[:, at] = more if k == 0 else product[:, at] + more
            return 0

        lax.fori_loop(0, LANES // CHUNK, part, 0)

    def wait_weights():
        for copy in w_handed:
            copy.wait_recv()

    plan, whole = gather_plan(n_ref, t, x, c)
    first = [(8.0, [], hand_weights), (0.0, whole[0], wait_weights)]
    sent = plan.run(copies, first + [(0.0, whole[k], functools.partial(use_block, k)) for k in (0, 1, -1, 2)])
    sent += moved + handed + scaled
    swap_sq = copies.start(sq, other_sq, sibling)

    def right_part(xx, total):
        swap_copy(0, xx).wait_recv()
        part = features(xx)
        right = MIXING * (image[:, part] + other[0, :, part])
        squared = jnp.where(core == 1, sq[:, part], other_sq[:, part])
        for m in range(MODELS):
            right = right + (1.0 - MIXING) * squared[m : m + 1] * wbuf[m, :, part].astype(F32)
        diagonal[0:1, part] = (1.0 - MIXING) * jnp.sum(squared, axis=0, keepdims=True)
        direction[:, part] = right
        residual[:, part] = right
        d2[:, part] = split(right)
        return total + fold_lanes(right * right)

    def spread_out(v):
        return jnp.broadcast_to(jnp.sum(v, axis=1, keepdims=True), (COLS, 128))

    def block_copy(k, source, target, first):
        to = lax.rem(chip + k, 16)
        to = lax.div(to, 4) * 8 + lax.rem(to, 4) * 2 + core
        return pltpu.make_async_remote_copy(
            src_ref=source.at[to],
            dst_ref=target.at[chip],
            send_sem=out_send.at[first + k],
            recv_sem=out_recv.at[first + k],
            device_id=plane(k),
            device_id_type=MESH,
        )

    def send_blocks(values, source, target, first):
        def cut(group, _):
            value = values(pl.ds(pl.multiple_of(group * 640, 128), 640))
            for k in range(4):
                source[group * 4 + k, :, 0:160] = value[:, 160 * k : 160 * k + 160].astype(source.dtype)
            return 0

        def send_one(k, _):
            block_copy(k, source, target, first).start()
            return 0

        lax.fori_loop(0, 8, cut, 0)
        target[chip] = source[x * 8 + t]
        lax.fori_loop(1, 16, send_one, 0)

    def solve_step(step, _):
        @pl.when(step == 0)
        def _():
            slot = slots(0, LANES)
            outputs = jnp.zeros((COLS, LANES), F32)
            first = jnp.int32(0)
            for m in range(MODELS):
                size = len_ref[m]
                mask = jnp.where((slot >= first) & (slot < first + size), 1.0, 0.0)
                first = first + size
                outputs = outputs + mask * product[COLS * m : COLS * m + COLS, :]
            ub[:COLS] = outputs.astype(BF16)
            ub[COLS:] = jnp.zeros((COLS, LANES), BF16)

        @pl.when(step > 0)
        def _():
            total = jnp.zeros((2 * COLS, LANES), F32)
            for xx in range(4):
                total = total + dot(d2[:, 1280 * xx : 1280 * xx + 1280], block_of(xx))
            projected = fold(total) * jnp.where(slots(0, LANES) < LIVE, 1.0, 0.0)
            norm[step] = spread_out(fold_lanes(projected * projected))
            norm_copy(step).start()
            ub[...] = split(projected)

        @pl.when(step < ITERS)
        def _():
            for xx in range(4):
                image[:, 1280 * xx : 1280 * xx + 1280] = fold(dot(ub[...], turned[xx]))
                swap_copy(step, xx).start()

        @pl.when(step == 0)
        def _():
            swap_sq.wait()
            squared_norm[...] = spread_out(each(right_part, jnp.zeros((COLS, 128), F32)))
            merged[...] = jnp.zeros_like(merged)

        @pl.when(step > 0)
        def _():
            def weighted(xx, total):
                now = direction[:, features(xx)]
                return total + fold_lanes(diagonal[0:1, features(xx)] * now * now)

            inner = spread_out(each(weighted, jnp.zeros((COLS, 128), F32)))
            norm_copy(step).wait()
            curvature = MIXING * (norm[step] + other_norm[step]) + inner
            size[...] = squared_norm[...] / curvature

        @pl.when((step > 0) & (step < ITERS))
        def _():
            factor = size[:, :1]
            merged[...] += factor * direction[...]

            @pl.when(step == ITERS - 1)
            def _():
                send_blocks(lambda part: merged[:, part], blocks, landed, 0)

            def residual_part(xx, total):
                part = features(xx)
                swap_copy(step, xx).wait_recv()
                full = MIXING * (image[:, part] + other[step, :, part]) + diagonal[0:1, part] * direction[:, part]
                rest = residual[:, part] - factor * full
                residual[:, part] = rest
                return total + fold_lanes(rest * rest)

            norm_next = spread_out(each(residual_part, jnp.zeros((COLS, 128), F32)))
            ratio = (norm_next / squared_norm[...])[:, :1]
            squared_norm[...] = norm_next

            def direction_part(xx, _):
                part = features(xx)
                now = residual[:, part] + ratio * direction[:, part]
                direction[:, part] = now
                d2[:, part] = split(now)
                return 0

            each(direction_part)

        @pl.when(step < ITERS)
        def _():
            def sent_part(xx, _):
                swap_copy(step, xx).wait_send()
                return 0

            each(sent_part)

        return 0

    lax.fori_loop(0, ITERS + 1, solve_step, 0)
    send_blocks(lambda part: size[:, :1] * direction[:, part], last_blocks, last_landed, 16)

    def wait_blocks(k, _):
        block_copy(k, blocks, landed, 0).wait()
        block_copy(k, last_blocks, last_landed, 16).wait()
        return 0

    lax.fori_loop(1, 16, wait_blocks, 0)
    result = landed[...] + last_landed[...].astype(F32)
    out_ref[...] = result.reshape(256, 256).T[:160]
    for copy in sent + w_moved + w_handed:
        copy.wait_send()


def body(hidden, gains, weights, lengths):
    vmem = pl.BlockSpec(memory_space=pltpu.VMEM)
    wide = (COLS, WIDTH)
    count = 250
    return pl.pallas_call(
        solve_kernel,
        out_shape=jax.ShapeDtypeStruct((160, 256), F32),
        in_specs=[vmem, vmem, vmem, pl.BlockSpec(memory_space=pltpu.SMEM)],
        out_specs=vmem,
        scratch_shapes=[
            pltpu.VMEM((32, 8, 128), F32),
            pltpu.VMEM((MODELS, 8, 128), F32),
            pltpu.VMEM((2, 80, 512), BF16),
            pltpu.VMEM((MODELS, 80, 512), BF16),
            pltpu.VMEM((16, COLS, 1280), BF16),
            pltpu.VMEM((4, 2, 4, 2, 5, 16, LANES), BF16),
            pltpu.VMEM((MODELS, COLS, WIDTH), BF16),
            pltpu.VMEM((2 * COLS, WIDTH), BF16),
            pltpu.VMEM(wide, F32),
            pltpu.VMEM((MODELS, WIDTH), F32),
            pltpu.VMEM((ITERS, COLS, WIDTH), F32),
            pltpu.VMEM((MODELS, WIDTH), F32),
            pltpu.VMEM((ITERS + 1, COLS, 128), F32),
            pltpu.VMEM((ITERS + 1, COLS, 128), F32),
            pltpu.VMEM(wide, F32),
            pltpu.VMEM(wide, F32),
            pltpu.VMEM(wide, F32),
            pltpu.VMEM((8, WIDTH), F32),
            pltpu.VMEM((COLS, 128), F32),
            pltpu.VMEM((COLS, 128), F32),
            pltpu.VMEM((2 * COLS, LANES), BF16),
            pltpu.VMEM((MODELS * COLS, LANES), F32),
            pltpu.VMEM((4, LANES, 1280), BF16),
            pltpu.VMEM((32, COLS, 256), F32),
            pltpu.VMEM((16, COLS, 256), F32),
            pltpu.VMEM((32, COLS, 256), BF16),
            pltpu.VMEM((16, COLS, 256), BF16),
            pltpu.SemaphoreType.DMA((32,)),
            pltpu.SemaphoreType.DMA((32,)),
            pltpu.SemaphoreType.DMA((4 * ITERS,)),
            pltpu.SemaphoreType.DMA((4 * ITERS,)),
            pltpu.SemaphoreType.DMA((ITERS + 1,)),
            pltpu.SemaphoreType.DMA((ITERS + 1,)),
            pltpu.SemaphoreType.DMA((32,)),
            pltpu.SemaphoreType.DMA((32,)),
            pltpu.SemaphoreType.DMA((count,)),
            pltpu.SemaphoreType.DMA((count,)),
        ],
        compiler_params=pltpu.CompilerParams(
            collective_id=0, has_side_effects=True, vmem_limit_bytes=56 * 2**20
        ),
    )(hidden.T, gains, weights[0], lengths)


def solution(mesh):
    return jax.shard_map(
        body,
        mesh=mesh,
        in_specs=(P("tok", ("row", "col")), P("tok", ("row", "col")), P("tok", "row", "col"), P()),
        out_specs=P(("row", "tok"), "col"),
        check_vma=False,
    )
```

```python
import functools

import jax
import jax.numpy as jnp
from jax import lax
from jax.experimental import pallas as pl
from jax.experimental.pallas import tpu as pltpu
from jax.sharding import PartitionSpec as P

MESH = pl.DeviceIdType.MESH
F32, BF16 = jnp.float32, jnp.bfloat16
WIDTH = 5120
EPSILON = 1e-06
MIXING = 0.9
ITERS = 4
MODELS = 8
QUART = 640
LANES = 2 * QUART
LIVE = 2304
CHUNK = 256
COLS = 16


def dot(a, b):
    return jnp.dot(a, b, preferred_element_type=F32)


def dot_nt(a, b):
    return lax.dot_general(a, b, (((1,), (1,)), ((), ())), preferred_element_type=F32)


def place():
    t = lax.axis_index("tok")
    x = lax.axis_index("row")
    c = lax.axis_index("col")
    return t, x, c


class Copies:
    def __init__(self, send, recv):
        self.send, self.recv, self.n = send, recv, 0

    def start(self, src, dst, device):
        copy = pltpu.make_async_remote_copy(
            src_ref=src,
            dst_ref=dst,
            send_sem=self.send.at[self.n],
            recv_sem=self.recv.at[self.n],
            device_id=device,
            device_id_type=MESH,
        )
        self.n += 1
        copy.start()
        return copy


class Plan:
    RATE, HOP = 45e3, 2.3

    def __init__(self):
        self.tasks, self.level = [], []

    def add(self, ref, device, link, size, deps, hops=1, level=0):
        self.tasks.append((ref, device, link, size, tuple(deps), hops))
        self.level.append(level)
        return len(self.tasks) - 1

    def ring(self, ref, device, axis, n, size, deps, way, level=0, far_level=None):
        deps, far_level = list(deps), level if far_level is None else far_level
        right = [self.add(ref(0), device(1), axis + "+", size, deps, 1, level)]
        left = [self.add(ref(0), device(-1), axis + "-", size, deps, 1, level)]
        for k in range(1, n // 2 - 1):
            right.append(self.add(ref(-k), device(1), axis + "+", size, right[-1:], 1, level))
            left.append(self.add(ref(k), device(-1), axis + "-", size, left[-1:], 1, level))
        last = n // 2 - 1
        if way == 0:
            far = self.add(ref(-last), device(1), axis + "+", size, right[-1:], 1, far_level)
        else:
            far = self.add(ref(last), device(-1), axis + "-", size, left[-1:], 1, far_level)
        arrived = {0: deps, n // 2: [far]}
        for k in range(1, n // 2):
            arrived[-k] = [right[k - 1]]
            arrived[k] = [left[k - 1]]
        return arrived

    def straight(self, ref, device, axis, n, size, deps):
        arrived = {0: list(deps)}
        for k in sorted(range(1 - n // 2, n // 2 + 1), key=abs):
            if k:
                link = axis + ("-" if k < 0 else "+")
                one = self.add(ref(0), device(k), link, size * abs(k), deps, abs(k))
                arrived[k if k == n // 2 else -k] = [one]
        return arrived

    def order(self):
        count = len(self.tasks)
        rank = [0.0] * count
        for i in reversed(range(count)):
            _, _, _, size, deps, hops = self.tasks[i]
            rank[i] += size / self.RATE + self.HOP + 0.7 * (hops - 1)
            for d in deps:
                rank[d] = max(rank[d], rank[i])
        free, arrival, placed, begins = {}, {}, [], {}
        while len(placed) < count:
            ready = {}
            for i, (_, _, link, _, deps, _) in enumerate(self.tasks):
                if i not in arrival and all(d in arrival for d in deps):
                    ready[i] = max([arrival[d] for d in deps] + [free.get(link, 0.0)])
            first = min(ready, key=lambda i: (round(ready[i], 3), self.level[i], -rank[i], i))
            _, _, link, size, _, hops = self.tasks[first]
            begins[first] = ready[first]
            free[link] = ready[first] + size / self.RATE
            arrival[first] = free[link] + self.HOP + 0.7 * (hops - 1)
            placed.append(first)
        return placed, arrival, begins

    def run(self, copies, extra):
        placed, arrival, begins = self.order()
        extra = [(at + max([arrival[d] for d in deps], default=0.0), deps, call) for at, deps, call in extra]
        extra = sorted(extra, key=lambda e: e[0])
        started, waited = {}, set()

        def wait(ids):
            for i in sorted(ids, key=arrival.get):
                if i not in waited:
                    waited.add(i)
                    started[i].wait_recv()

        def due(now):
            while extra and extra[0][0] + 0.5 <= now:
                _, deps, call = extra.pop(0)
                wait(deps)
                call()

        for i in placed:
            ref, device, _, _, deps, _ = self.tasks[i]
            due(begins[i])
            wait(deps)
            started[i] = copies.start(ref, ref, device)
        due(1e9)
        wait(arrival)
        return [started[i] for i in placed]


def gather_plan(n_ref, t, x, c):
    core = lax.rem(t, 2)
    y, z = lax.rem(c, 4), lax.div(c, 4) * 4 + lax.div(t, 2)
    every = slice(None)
    plan = Plan()
    unit = 16 * 128 * 2

    def xx(k):
        return lax.rem(x + k + 4, 4)

    def yy(k):
        return lax.rem(y + k + 4, 4)

    def at_x(k):
        return {"row": xx(k)}

    def at_y(k):
        return {"col": lax.div(c, 4) * 4 + yy(k)}

    def at_z(k):
        zz = lax.rem(z + k + 8, 8)
        return {"tok": lax.rem(zz, 4) * 2 + core, "col": lax.div(zz, 4) * 4 + y}

    def zpos(k, first, tiles):
        zz = lax.rem(z + k + 8, 8)
        start = lax.rem(zz, 2) * QUART + first * 128
        lanes = pl.ds(pl.multiple_of(start, 128), tiles * 128)
        return lax.div(zz, 4), lax.rem(lax.div(zz, 2), 2), lanes

    rows_ab, rows_c = pl.ds(0, 3), pl.ds(3, 2)
    size_a, size_b, size_c = 6 * unit, 9 * unit, 10 * unit

    def part_a(kx, ky, kz):
        h, f, l = zpos(kz, 0, 2)
        return n_ref.at[every if kx is None else xx(kx), h, every if ky is None else yy(ky), f, rows_ab, every, l]

    def part_b(kx, ky, kz):
        h, f, l = zpos(kz, 2, 3)
        return n_ref.at[every if kx is None else xx(kx), h, every if ky is None else yy(ky), f, rows_ab, every, l]

    def part_c(kx, ky, kz):
        if kz is None:
            return n_ref.at[xx(kx), every, yy(ky), every, rows_c, every, every]
        h, f, l = zpos(kz, 0, 5)
        return n_ref.at[every if kx is None else xx(kx), h, yy(ky), f, rows_c, every, l]

    def all_of(arrived):
        return [i for ids in arrived.values() for i in ids]

    b1 = plan.straight(lambda k: part_b(0, k, 0), at_y, "y", 4, size_b, [])
    c1 = plan.ring(lambda k: part_c(0, 0, k), at_z, "z", 8, size_c, [], 1)
    a1 = plan.straight(lambda k: part_a(k, 0, 0), at_x, "x", 4, size_a, [])
    b2 = plan.ring(lambda k: part_b(0, None, k), at_z, "z", 8, 4 * size_b, all_of(b1), 0)
    a2 = plan.ring(lambda k: part_a(None, k, 0), at_y, "y", 4, 4 * size_a, all_of(a1), 1)
    turns = ((0, 0), (1, 1), (-1, 1), (2, 2))
    whole = {0: all_of(b2), 1: [], -1: [], 2: []}
    c2 = {}
    for way, k in enumerate((0, 1, -1, 2, -2, 3, -3, 4)):
        c2[k] = plan.ring(lambda kx, k=k: part_c(kx, 0, k), at_x, "x", 4, size_c, c1[k], way % 2)
    for way, (k, level) in enumerate(turns):
        for kz in (0, 1, -1, 2, -2, 3, -3, 4):
            got = plan.ring(
                lambda ky, k=k, kz=kz: part_c(k, ky, kz), at_y, "y", 4, size_c, c2[kz][k], way % 2, level
            )
            whole[k] += all_of(got)
    for way, k in enumerate((0, 1, -1, 2, -2, 3, -3, 4)):
        got = plan.ring(
            lambda kx, k=k: part_b(kx, None, k), at_x, "x", 4, 4 * size_b, b2[k], way % 2, 1, 2
        )
        for kx in (1, -1, 2):
            whole[kx] += got[kx]
    for way, (k, level) in enumerate(turns):
        got = plan.ring(
            lambda kz, k=k: part_a(k, None, kz), at_z, "z", 8, 4 * size_a, all_of(a2), way % 2, level
        )
        whole[k] += all_of(got)
    return plan, whole


def split(v):
    high = v.astype(BF16)
    low = (v - high.astype(F32)).astype(BF16)
    return jnp.concatenate([high, low], axis=0)


def fold(v):
    return v[:COLS] + v[COLS:]


def row_of(tile):
    return jnp.concatenate([tile[k : k + 1] for k in range(4)], axis=1)


def solve_kernel(
    h_ref, g_ref, w_ref, len_ref, out_ref,
    sums, scales, halves, pieces, wt, n_ref, wbuf, d2, image, sq, other, other_sq, norm, other_norm, direction, residual,
    merged, diagonal, squared_norm, size, weighted, ub, product, turned, blocks, landed, last_blocks, last_landed, sq_send, sq_recv,
    swap_send, swap_recv, norm_send, norm_recv, out_send, out_recv, send, recv,
):
    t, x, c = place()
    core, zl = lax.rem(t, 2), lax.div(t, 2)
    zh, y = lax.div(c, 4), lax.rem(c, 4)
    chip, me = x * 4 + zl, x * 8 + c
    sibling = {"tok": zl * 2 + 1 - core}

    def plane(k):
        target = lax.rem(chip + k, 16)
        return {"row": lax.div(target, 4), "tok": lax.rem(target, 4) * 2 + core}

    def block(k):
        target = lax.rem(me + k, 32)
        return {"row": lax.div(target, 8), "col": lax.rem(target, 8)}

    def line(k, side):
        return {"tok": lax.rem(zl + k, 4) * 2 + side}

    barrier = pltpu.get_barrier_semaphore()

    def greet(device):
        pl.semaphore_signal(barrier, inc=1, device_id=device, device_id_type=MESH)

    def greet_block(k, _):
        greet(block(k))
        return 0

    lax.fori_loop(1, 32, greet_block, 0)
    for k in range(1, 4):
        zz = lax.rem(zl + k, 4)
        greet(line(k, core))
        greet(line(k, 1 - core))
        greet({"tok": zz * 2 + core, "col": (1 - zh) * 4 + y})
        for kx in range(1, 4):
            greet({"row": lax.rem(x + kx, 4), "tok": zz * 2 + core})
    greet(sibling)

    h = h_ref[...].astype(F32)
    squares = jnp.sum(h * h, axis=0, keepdims=True)
    sums[me] = jnp.zeros((8, 128), F32)
    for k in range(4):
        sums[me, k : k + 1, :] = squares[:, 128 * k : 128 * k + 128]
    halves[0] = h_ref[:80]
    halves[1] = h_ref[80:]
    scales[t] = jnp.zeros((8, 128), F32)
    scales[t, 4:5, 0:80] = g_ref[:, 0:80]
    scales[t, 5:6, 0:80] = g_ref[:, 80:160]
    mine = lax.div(zl, 2)
    pieces[t] = halves[mine]
    blocks[...] = jnp.zeros_like(blocks)
    last_blocks[...] = jnp.zeros_like(last_blocks)
    pl.semaphore_wait(barrier, 50)

    def sums_copy(k):
        return pltpu.make_async_remote_copy(
            src_ref=sums.at[me],
            dst_ref=sums.at[me],
            send_sem=sq_send.at[k],
            recv_sem=sq_recv.at[k],
            device_id=block(k),
            device_id_type=MESH,
        )

    def send_sums(k, _):
        sums_copy(k).start()
        return 0

    def wait_sums(k, _):
        sums_copy(k).wait()
        return 0

    lax.fori_loop(1, 32, send_sums, 0)

    copies = Copies(send, recv)
    moved = []
    for k in range(1, 4):
        target = lax.rem(zl + k, 4)
        moved.append(copies.start(halves.at[lax.div(target, 2)], pieces.at[t], line(k, core)))
    handed = [copies.start(pieces.at[t], pieces.at[t], sibling)]

    eye = lax.broadcasted_iota(jnp.int32, (256, 256), 0) == lax.broadcasted_iota(jnp.int32, (256, 256), 1)
    eye = jnp.where(eye, 1.0, 0.0).astype(BF16)
    wt[...] = dot_nt(eye, w_ref[...]).astype(BF16).reshape(16, COLS, 1280)

    def w_lanes(k):
        return pl.ds(pl.multiple_of(lax.rem(lax.div(chip + 16 - k, 4), 4) * 1280, 128), 1280)

    def w_slot(k):
        return wbuf.at[lax.rem(chip + 16 - k, 4) * 2 + core, :, w_lanes(k)]

    wbuf[t, :, w_lanes(0)] = wt[chip]
    w_moved, w_handed = [], []

    def send_weights():
        for k in range(1, 16):
            w_moved.append(copies.start(wt.at[lax.rem(chip + k, 16)], w_slot(0), plane(k)))
        w_handed.append(copies.start(w_slot(0), w_slot(0), sibling))

    def hand_weights():
        for k in range(1, 16):
            w_moved[k - 1].wait_recv()
            w_handed.append(copies.start(w_slot(k), w_slot(k), sibling))

    lax.fori_loop(1, 32, wait_sums, 0)
    inverse = lax.rsqrt(jnp.sum(sums[...], axis=0) / WIDTH + EPSILON)
    slot = lax.broadcasted_iota(jnp.int32, (8, 128), 0) * 128 + lax.broadcasted_iota(jnp.int32, (8, 128), 1)
    live = (slot < len_ref[t]).astype(F32)
    scales[t, 0:4, :] = (inverse * live)[0:4]
    scaled = [copies.start(scales.at[t], scales.at[t], sibling)]
    for k in range(1, 4):
        scaled.append(copies.start(scales.at[t], scales.at[t], line(k, core)))
        scaled.append(copies.start(scales.at[t], scales.at[t], line(k, 1 - core)))
    send_weights()
    for k in range(1, 4):
        moved[k - 1].wait_recv()
        model = lax.rem(zl + 4 - k, 4) * 2 + core
        handed.append(copies.start(pieces.at[model], pieces.at[model], sibling))
    for copy in scaled + handed:
        copy.wait_recv()

    window = lax.rem(t, 4) * QUART
    shift = lax.broadcasted_iota(jnp.int32, (512, QUART), 0)
    shift = shift - lax.broadcasted_iota(jnp.int32, (512, QUART), 1)
    spread = lax.broadcasted_iota(jnp.int32, (80, 128), 0) == lax.broadcasted_iota(jnp.int32, (80, 128), 1)

    lane = lax.broadcasted_iota(jnp.int32, (80, 128), 1)

    def add_model(m, carry):
        acc, tile, first = carry
        size = len_ref[m]
        scale = scales[m]
        gain = jnp.where(mine == 0, scale[4:5], scale[5:6])
        gain = jnp.sum(jnp.where(spread, gain, 0.0), axis=1, keepdims=True)
        normed = (pieces[m].astype(F32) * row_of(scale) * gain).astype(BF16)
        pick = jnp.where(shift == window - first, 1.0, 0.0).astype(BF16)
        wide_normed = normed.astype(F32)
        total = jnp.sum(wide_normed * wide_normed, axis=1, keepdims=True)
        tile = jnp.where(lax.rem(lane, 8) == m, total, tile)
        return acc + dot(normed, pick), tile, first + size

    carry = (jnp.zeros((80, QUART), F32), jnp.zeros((80, 128), F32), jnp.int32(0))
    for m in range(MODELS):
        carry = add_model(m, carry)
    acc, tile, _ = carry
    high = tile.astype(BF16).astype(F32)
    middle = (tile - high).astype(BF16).astype(F32)
    tile = jnp.where(lane < 8, high, jnp.where(lane < 16, middle, tile - high - middle))
    tile = jnp.where(lane < 24, tile, 0.0)
    acc = jnp.concatenate([acc[:, :512], acc[:, 512:] + jnp.where(lax.rem(t, 4) == 3, tile, 0.0)], axis=1)
    lanes = pl.ds(pl.multiple_of(lax.rem(zl, 2) * QUART, 128), QUART)
    n_ref[x, zh, y, mine, :, :, lanes] = acc.astype(BF16).reshape(5, 16, QUART)

    def block_of(xx):
        return n_ref[xx].reshape(1280, LANES)

    def features(xx):
        return pl.ds(xx * 1280 if isinstance(xx, int) else pl.multiple_of(xx * 1280, 128), 1280)

    def each(body, init=0):
        for xx in range(4):
            init = body(xx, init)
        return init

    def fold_lanes(v):
        return functools.reduce(jnp.add, [v[:, 128 * k : 128 * k + 128] for k in range(10)])

    def swap_copy(slot, xx):
        return pltpu.make_async_remote_copy(
            src_ref=image.at[:, features(xx)],
            dst_ref=other.at[slot, :, features(xx)],
            send_sem=swap_send.at[slot * 4 + xx],
            recv_sem=swap_recv.at[slot * 4 + xx],
            device_id=sibling,
            device_id_type=MESH,
        )

    def norm_copy(step):
        return pltpu.make_async_remote_copy(
            src_ref=norm.at[step],
            dst_ref=other_norm.at[step],
            send_sem=norm_send.at[step],
            recv_sem=norm_recv.at[step],
            device_id=sibling,
            device_id_type=MESH,
        )

    def slots(first, count):
        at = lax.broadcasted_iota(jnp.int32, (1, count), 1) + first
        return at + core * QUART + jnp.where(at >= QUART, QUART, 0)

    take = lax.broadcasted_iota(jnp.int32, (16, 128), 1)
    take = (lax.rem(take, 8) == lax.broadcasted_iota(jnp.int32, (16, 128), 0)) & (take < 24)
    take = jnp.where(take, 1.0, 0.0).astype(BF16)

    def use_block(k, step):
        xx = lax.rem(x + k + 4, 4)
        if step == 0:
            spare = n_ref[xx, :, :, :, :, :, LANES - 128 :].reshape(1280, 128)
            sq[:, features(xx)] = dot_nt(take, spare)[:MODELS]
        weights = wbuf[:, :, features(xx)].reshape(MODELS * COLS, 1280)
        at = slice(CHUNK * step, CHUNK * step + CHUNK)
        block = n_ref[xx, :, :, :, :, :, at].reshape(1280, CHUNK)
        turned[xx, at, :] = block.T
        more = dot(weights, block)
        product[:, at] = more if k == 0 else product[:, at] + more

    def wait_weights():
        for copy in w_handed:
            copy.wait_recv()

    plan, whole = gather_plan(n_ref, t, x, c)
    first = [(8.0, [], hand_weights), (0.0, whole[0], wait_weights)]
    uses = [(1.0 * i, whole[k], functools.partial(use_block, k, i)) for k in (0, 1, -1, 2) for i in range(5)]
    sent = plan.run(copies, first + uses)
    sent += moved + handed + scaled
    swap_sq = copies.start(sq, other_sq, sibling)

    def right_part(xx, total):
        swap_copy(0, xx).wait_recv()
        part = features(xx)
        right = MIXING * (image[:, part] + other[0, :, part])
        squared = jnp.where(core == 1, sq[:, part], other_sq[:, part])
        for m in range(MODELS):
            right = right + (1.0 - MIXING) * squared[m : m + 1] * wbuf[m, :, part].astype(F32)
        diagonal[0:1, part] = (1.0 - MIXING) * jnp.sum(squared, axis=0, keepdims=True)
        direction[:, part] = right
        residual[:, part] = right
        d2[:, part] = split(right)
        length, inner = total
        return length + fold_lanes(right * right), inner + fold_lanes(diagonal[0:1, part] * right * right)

    def spread_out(v):
        return jnp.broadcast_to(jnp.sum(v, axis=1, keepdims=True), (COLS, 128))

    def block_copy(k, source, target, first):
        to = lax.rem(chip + k, 16)
        to = lax.div(to, 4) * 8 + lax.rem(to, 4) * 2 + core
        return pltpu.make_async_remote_copy(
            src_ref=source.at[to],
            dst_ref=target.at[chip],
            send_sem=out_send.at[first + k],
            recv_sem=out_recv.at[first + k],
            device_id=plane(k),
            device_id_type=MESH,
        )

    def send_blocks(values, source, target, first):
        def cut(group, _):
            value = values(pl.ds(pl.multiple_of(group * 640, 128), 640))
            for k in range(4):
                source[group * 4 + k, :, 0:160] = value[:, 160 * k : 160 * k + 160].astype(source.dtype)
            return 0

        def send_one(k, _):
            block_copy(k, source, target, first).start()
            return 0

        lax.fori_loop(0, 8, cut, 0)
        target[chip] = source[x * 8 + t]
        lax.fori_loop(1, 16, send_one, 0)

    def solve_step(step, _):
        @pl.when(step == 0)
        def _():
            slot = slots(0, LANES)
            outputs = jnp.zeros((COLS, LANES), F32)
            first = jnp.int32(0)
            for m in range(MODELS):
                size = len_ref[m]
                mask = jnp.where((slot >= first) & (slot < first + size), 1.0, 0.0)
                first = first + size
                outputs = outputs + mask * product[COLS * m : COLS * m + COLS, :]
            ub[:COLS] = outputs.astype(BF16)
            ub[COLS:] = jnp.zeros((COLS, LANES), BF16)

        @pl.when(step > 0)
        def _():
            total = jnp.zeros((2 * COLS, LANES), F32)
            for xx in range(4):
                total = total + dot(d2[:, 1280 * xx : 1280 * xx + 1280], block_of(xx))
            projected = fold(total) * jnp.where(slots(0, LANES) < LIVE, 1.0, 0.0)
            norm[step] = spread_out(fold_lanes(projected * projected))
            norm_copy(step).start()
            ub[...] = split(projected)

        @pl.when(step < ITERS)
        def _():
            for xx in range(5):
                if xx < 4:
                    image[:, 1280 * xx : 1280 * xx + 1280] = fold(dot(ub[...], turned[xx]))
                if xx > 0:
                    swap_copy(step, xx - 1).start()

        @pl.when(step == 0)
        def _():
            swap_sq.wait()
            zero = jnp.zeros((COLS, 128), F32)
            length, inner = each(right_part, (zero, zero))
            squared_norm[...], weighted[...] = spread_out(length), spread_out(inner)
            merged[...] = jnp.zeros_like(merged)

        @pl.when(step > 0)
        def _():
            norm_copy(step).wait()
            curvature = MIXING * (norm[step] + other_norm[step]) + weighted[...]
            size[...] = squared_norm[...] / curvature

        @pl.when((step > 0) & (step < ITERS))
        def _():
            factor = size[:, :1]
            merged[...] += factor * direction[...]

            @pl.when(step == ITERS - 1)
            def _():
                send_blocks(lambda part: merged[:, part], blocks, landed, 0)

            def residual_part(xx, total):
                part = features(xx)
                swap_copy(step, xx).wait_recv()
                full = MIXING * (image[:, part] + other[step, :, part]) + diagonal[0:1, part] * direction[:, part]
                rest = residual[:, part] - factor * full
                residual[:, part] = rest
                return total + fold_lanes(rest * rest)

            norm_next = spread_out(each(residual_part, jnp.zeros((COLS, 128), F32)))
            ratio = (norm_next / squared_norm[...])[:, :1]
            squared_norm[...] = norm_next

            def direction_part(xx, total):
                part = features(xx)
                now = residual[:, part] + ratio * direction[:, part]
                direction[:, part] = now
                d2[:, part] = split(now)
                return total + fold_lanes(diagonal[0:1, part] * now * now)

            weighted[...] = spread_out(each(direction_part, jnp.zeros((COLS, 128), F32)))

        @pl.when(step < ITERS)
        def _():
            def sent_part(xx, _):
                swap_copy(step, xx).wait_send()
                return 0

            each(sent_part)

        return 0

    lax.fori_loop(0, ITERS + 1, solve_step, 0)
    send_blocks(lambda part: size[:, :1] * direction[:, part], last_blocks, last_landed, 16)

    for copy in sent + w_moved + w_handed:
        copy.wait_send()

    def wait_blocks(k, _):
        block_copy(k, blocks, landed, 0).wait()
        block_copy(k, last_blocks, last_landed, 16).wait()
        return 0

    lax.fori_loop(1, 16, wait_blocks, 0)
    result = landed[...] + last_landed[...].astype(F32)
    out_ref[...] = result.reshape(256, 256).T[:160]


def body(hidden, gains, weights, lengths):
    vmem = pl.BlockSpec(memory_space=pltpu.VMEM)
    wide = (COLS, WIDTH)
    count = 250
    return pl.pallas_call(
        solve_kernel,
        out_shape=jax.ShapeDtypeStruct((160, 256), F32),
        in_specs=[vmem, vmem, vmem, pl.BlockSpec(memory_space=pltpu.SMEM)],
        out_specs=vmem,
        scratch_shapes=[
            pltpu.VMEM((32, 8, 128), F32),
            pltpu.VMEM((MODELS, 8, 128), F32),
            pltpu.VMEM((2, 80, 512), BF16),
            pltpu.VMEM((MODELS, 80, 512), BF16),
            pltpu.VMEM((16, COLS, 1280), BF16),
            pltpu.VMEM((4, 2, 4, 2, 5, 16, LANES), BF16),
            pltpu.VMEM((MODELS, COLS, WIDTH), BF16),
            pltpu.VMEM((2 * COLS, WIDTH), BF16),
            pltpu.VMEM(wide, F32),
            pltpu.VMEM((MODELS, WIDTH), F32),
            pltpu.VMEM((ITERS, COLS, WIDTH), F32),
            pltpu.VMEM((MODELS, WIDTH), F32),
            pltpu.VMEM((ITERS + 1, COLS, 128), F32),
            pltpu.VMEM((ITERS + 1, COLS, 128), F32),
            pltpu.VMEM(wide, F32),
            pltpu.VMEM(wide, F32),
            pltpu.VMEM(wide, F32),
            pltpu.VMEM((8, WIDTH), F32),
            pltpu.VMEM((COLS, 128), F32),
            pltpu.VMEM((COLS, 128), F32),
            pltpu.VMEM((COLS, 128), F32),
            pltpu.VMEM((2 * COLS, LANES), BF16),
            pltpu.VMEM((MODELS * COLS, LANES), F32),
            pltpu.VMEM((4, LANES, 1280), BF16),
            pltpu.VMEM((32, COLS, 256), F32),
            pltpu.VMEM((16, COLS, 256), F32),
            pltpu.VMEM((32, COLS, 256), BF16),
            pltpu.VMEM((16, COLS, 256), BF16),
            pltpu.SemaphoreType.DMA((32,)),
            pltpu.SemaphoreType.DMA((32,)),
            pltpu.SemaphoreType.DMA((4 * ITERS,)),
            pltpu.SemaphoreType.DMA((4 * ITERS,)),
            pltpu.SemaphoreType.DMA((ITERS + 1,)),
            pltpu.SemaphoreType.DMA((ITERS + 1,)),
            pltpu.SemaphoreType.DMA((32,)),
            pltpu.SemaphoreType.DMA((32,)),
            pltpu.SemaphoreType.DMA((count,)),
            pltpu.SemaphoreType.DMA((count,)),
        ],
        compiler_params=pltpu.CompilerParams(
            collective_id=0, has_side_effects=True, vmem_limit_bytes=56 * 2**20
        ),
    )(hidden.T, gains, weights[0], lengths)


def solution(mesh):
    return jax.shard_map(
        body,
        mesh=mesh,
        in_specs=(P("tok", ("row", "col")), P("tok", ("row", "col")), P("tok", "row", "col"), P()),
        out_specs=P(("row", "tok"), "col"),
        check_vma=False,
    )
```

```python
import functools

import jax
import jax.numpy as jnp
from jax import lax
from jax.experimental import pallas as pl
from jax.experimental.pallas import tpu as pltpu
from jax.sharding import PartitionSpec as P

MESH = pl.DeviceIdType.MESH
F32, BF16 = jnp.float32, jnp.bfloat16
WIDTH = 5120
EPSILON = 1e-06
MIXING = 0.9
ITERS = 4
MODELS = 8
QUART = 640
LANES = 2 * QUART
LIVE = 2304
CHUNK = 256
COLS = 16


def dot(a, b):
    return jnp.dot(a, b, preferred_element_type=F32)


def dot_nt(a, b):
    return lax.dot_general(a, b, (((1,), (1,)), ((), ())), preferred_element_type=F32)


def place():
    t = lax.axis_index("tok")
    x = lax.axis_index("row")
    c = lax.axis_index("col")
    return t, x, c


class Copies:
    def __init__(self, send, recv):
        self.send, self.recv, self.n = send, recv, 0

    def start(self, src, dst, device):
        copy = pltpu.make_async_remote_copy(
            src_ref=src,
            dst_ref=dst,
            send_sem=self.send.at[self.n],
            recv_sem=self.recv.at[self.n],
            device_id=device,
            device_id_type=MESH,
        )
        self.n += 1
        copy.start()
        return copy


class Plan:
    RATE, HOP = 42e3, 3.0

    def __init__(self):
        self.tasks, self.level = [], []

    def add(self, ref, device, link, size, deps, hops=1, level=0):
        self.tasks.append((ref, device, link, size, tuple(deps), hops))
        self.level.append(level)
        return len(self.tasks) - 1

    def ring(self, ref, device, axis, n, size, deps, way, level=0, far_level=None):
        deps, far_level = list(deps), level if far_level is None else far_level
        right = [self.add(ref(0), device(1), axis + "+", size, deps, 1, level)]
        left = [self.add(ref(0), device(-1), axis + "-", size, deps, 1, level)]
        for k in range(1, n // 2 - 1):
            right.append(self.add(ref(-k), device(1), axis + "+", size, right[-1:], 1, level))
            left.append(self.add(ref(k), device(-1), axis + "-", size, left[-1:], 1, level))
        last = n // 2 - 1
        if way == 0:
            far = self.add(ref(-last), device(1), axis + "+", size, right[-1:], 1, far_level)
        else:
            far = self.add(ref(last), device(-1), axis + "-", size, left[-1:], 1, far_level)
        arrived = {0: deps, n // 2: [far]}
        for k in range(1, n // 2):
            arrived[-k] = [right[k - 1]]
            arrived[k] = [left[k - 1]]
        return arrived

    def straight(self, ref, device, axis, n, size, deps):
        arrived = {0: list(deps)}
        for k in sorted(range(1 - n // 2, n // 2 + 1), key=abs):
            if k:
                link = axis + ("-" if k < 0 else "+")
                one = self.add(ref(0), device(k), link, size * abs(k), deps, abs(k))
                arrived[k if k == n // 2 else -k] = [one]
        return arrived

    def order(self):
        count = len(self.tasks)
        rank = [0.0] * count
        for i in reversed(range(count)):
            _, _, _, size, deps, hops = self.tasks[i]
            rank[i] += size / self.RATE + self.HOP + 0.7 * (hops - 1)
            for d in deps:
                rank[d] = max(rank[d], rank[i])
        free, arrival, placed, begins = {}, {}, [], {}
        while len(placed) < count:
            ready = {}
            for i, (_, _, link, _, deps, _) in enumerate(self.tasks):
                if i not in arrival and all(d in arrival for d in deps):
                    ready[i] = max([arrival[d] for d in deps] + [free.get(link, 0.0)])
            first = min(ready, key=lambda i: (round(ready[i], 3), self.level[i], -rank[i], i))
            _, _, link, size, _, hops = self.tasks[first]
            begins[first] = ready[first]
            free[link] = ready[first] + size / self.RATE
            arrival[first] = free[link] + self.HOP + 0.7 * (hops - 1)
            placed.append(first)
        return placed, arrival, begins

    def run(self, copies, extra):
        placed, arrival, begins = self.order()
        extra = [(at + max([arrival[d] for d in deps], default=0.0), deps, call) for at, deps, call in extra]
        extra = sorted(extra, key=lambda e: e[0])
        started, waited = {}, set()

        def wait(ids):
            for i in sorted(ids, key=arrival.get):
                if i not in waited:
                    waited.add(i)
                    started[i].wait_recv()

        def due(now):
            while extra and extra[0][0] + 0.5 <= now:
                _, deps, call = extra.pop(0)
                wait(deps)
                call()

        for i in placed:
            ref, device, _, _, deps, _ = self.tasks[i]
            due(begins[i])
            wait(deps)
            started[i] = copies.start(ref, ref, device)
        due(1e9)
        wait(arrival)
        return [started[i] for i in placed]


def gather_plan(n_ref, t, x, c):
    core = lax.rem(t, 2)
    y, z = lax.rem(c, 4), lax.div(c, 4) * 4 + lax.div(t, 2)
    every = slice(None)
    plan = Plan()
    unit = 16 * 128 * 2

    def xx(k):
        return lax.rem(x + k + 4, 4)

    def yy(k):
        return lax.rem(y + k + 4, 4)

    def at_x(k):
        return {"row": xx(k)}

    def at_y(k):
        return {"col": lax.div(c, 4) * 4 + yy(k)}

    def at_z(k):
        zz = lax.rem(z + k + 8, 8)
        return {"tok": lax.rem(zz, 4) * 2 + core, "col": lax.div(zz, 4) * 4 + y}

    def zpos(k, first, tiles):
        zz = lax.rem(z + k + 8, 8)
        start = lax.rem(zz, 2) * QUART + first * 128
        lanes = pl.ds(pl.multiple_of(start, 128), tiles * 128)
        return lax.div(zz, 4), lax.rem(lax.div(zz, 2), 2), lanes

    rows_ab, rows_c = pl.ds(0, 3), pl.ds(3, 2)
    size_a, size_b, size_c = 6 * unit, 9 * unit, 10 * unit

    def part_a(kx, ky, kz):
        h, f, l = zpos(kz, 0, 2)
        return n_ref.at[every if kx is None else xx(kx), h, every if ky is None else yy(ky), f, rows_ab, every, l]

    def part_b(kx, ky, kz):
        h, f, l = zpos(kz, 2, 3)
        return n_ref.at[every if kx is None else xx(kx), h, every if ky is None else yy(ky), f, rows_ab, every, l]

    def part_c(kx, ky, kz):
        if kz is None:
            return n_ref.at[xx(kx), every, yy(ky), every, rows_c, every, every]
        h, f, l = zpos(kz, 0, 5)
        return n_ref.at[every if kx is None else xx(kx), h, yy(ky), f, rows_c, every, l]

    def all_of(arrived):
        return [i for ids in arrived.values() for i in ids]

    b1 = plan.straight(lambda k: part_b(0, k, 0), at_y, "y", 4, size_b, [])
    c1 = plan.ring(lambda k: part_c(0, 0, k), at_z, "z", 8, size_c, [], 1)
    a1 = plan.straight(lambda k: part_a(k, 0, 0), at_x, "x", 4, size_a, [])
    b2 = plan.ring(lambda k: part_b(0, None, k), at_z, "z", 8, 4 * size_b, all_of(b1), 0)
    a2 = plan.ring(lambda k: part_a(None, k, 0), at_y, "y", 4, 4 * size_a, all_of(a1), 1)
    turns = ((0, 0), (1, 1), (-1, 1), (2, 2))
    whole = {0: all_of(b2), 1: [], -1: [], 2: []}
    c2 = {}
    for way, k in enumerate((0, 1, -1, 2, -2, 3, -3, 4)):
        c2[k] = plan.ring(lambda kx, k=k: part_c(kx, 0, k), at_x, "x", 4, size_c, c1[k], way % 2)
    for way, (k, level) in enumerate(turns):
        for kz in (0, 1, -1, 2, -2, 3, -3, 4):
            got = plan.ring(
                lambda ky, k=k, kz=kz: part_c(k, ky, kz), at_y, "y", 4, size_c, c2[kz][k], way % 2, level
            )
            whole[k] += all_of(got)
    for way, k in enumerate((0, 1, -1, 2, -2, 3, -3, 4)):
        got = plan.ring(
            lambda kx, k=k: part_b(kx, None, k), at_x, "x", 4, 4 * size_b, b2[k], way % 2, 1, 2
        )
        for kx in (1, -1, 2):
            whole[kx] += got[kx]
    for way, (k, level) in enumerate(turns):
        got = plan.ring(
            lambda kz, k=k: part_a(k, None, kz), at_z, "z", 8, 4 * size_a, all_of(a2), way % 2, level
        )
        whole[k] += all_of(got)
    return plan, whole


def split(v):
    high = v.astype(BF16)
    low = (v - high.astype(F32)).astype(BF16)
    return jnp.concatenate([high, low], axis=0)


def fold(v):
    return v[:COLS] + v[COLS:]


def row_of(tile):
    return jnp.concatenate([tile[k : k + 1] for k in range(4)], axis=1)


def solve_kernel(
    h_ref, g_ref, w_ref, len_ref, out_ref,
    sums, scales, halves, pieces, wt, n_ref, wbuf, d2, image, sq, other, other_sq, norm, other_norm, direction, residual,
    merged, diagonal, squared_norm, size, weighted, ub, product, turned, blocks, landed, last_blocks, last_landed, sq_send, sq_recv,
    swap_send, swap_recv, norm_send, norm_recv, out_send, out_recv, send, recv,
):
    t, x, c = place()
    core, zl = lax.rem(t, 2), lax.div(t, 2)
    zh, y = lax.div(c, 4), lax.rem(c, 4)
    chip, me = x * 4 + zl, x * 8 + c
    sibling = {"tok": zl * 2 + 1 - core}

    def plane(k):
        target = lax.rem(chip + k, 16)
        return {"row": lax.div(target, 4), "tok": lax.rem(target, 4) * 2 + core}

    def block(k):
        target = lax.rem(me + k, 32)
        return {"row": lax.div(target, 8), "col": lax.rem(target, 8)}

    def line(k, side):
        return {"tok": lax.rem(zl + k, 4) * 2 + side}

    barrier = pltpu.get_barrier_semaphore()

    def greet(device):
        pl.semaphore_signal(barrier, inc=1, device_id=device, device_id_type=MESH)

    def greet_block(k, _):
        greet(block(k))
        return 0

    lax.fori_loop(1, 32, greet_block, 0)
    for k in range(1, 4):
        zz = lax.rem(zl + k, 4)
        greet(line(k, core))
        greet(line(k, 1 - core))
        greet({"tok": zz * 2 + core, "col": (1 - zh) * 4 + y})
        for kx in range(1, 4):
            greet({"row": lax.rem(x + kx, 4), "tok": zz * 2 + core})
    greet(sibling)

    h = h_ref[...].astype(F32)
    squares = jnp.sum(h * h, axis=0, keepdims=True)
    sums[me] = jnp.zeros((8, 128), F32)
    for k in range(4):
        sums[me, k : k + 1, :] = squares[:, 128 * k : 128 * k + 128]
    halves[0] = h_ref[:80]
    halves[1] = h_ref[80:]
    scales[t] = jnp.zeros((8, 128), F32)
    scales[t, 4:5, 0:80] = g_ref[:, 0:80]
    scales[t, 5:6, 0:80] = g_ref[:, 80:160]
    mine = lax.div(zl, 2)
    pieces[t] = halves[mine]
    blocks[...] = jnp.zeros_like(blocks)
    last_blocks[...] = jnp.zeros_like(last_blocks)
    pl.semaphore_wait(barrier, 50)

    def sums_copy(k):
        return pltpu.make_async_remote_copy(
            src_ref=sums.at[me],
            dst_ref=sums.at[me],
            send_sem=sq_send.at[k],
            recv_sem=sq_recv.at[k],
            device_id=block(k),
            device_id_type=MESH,
        )

    def send_sums(k, _):
        sums_copy(k).start()
        return 0

    def wait_sums(k, _):
        sums_copy(k).wait_recv()
        return 0

    def wait_sums_sent(k, _):
        sums_copy(k).wait_send()
        return 0

    lax.fori_loop(1, 32, send_sums, 0)

    copies = Copies(send, recv)
    moved = []
    for k in range(1, 4):
        target = lax.rem(zl + k, 4)
        moved.append(copies.start(halves.at[lax.div(target, 2)], pieces.at[t], line(k, core)))
    handed = [copies.start(pieces.at[t], pieces.at[t], sibling)]

    eye = lax.broadcasted_iota(jnp.int32, (256, 256), 0) == lax.broadcasted_iota(jnp.int32, (256, 256), 1)
    eye = jnp.where(eye, 1.0, 0.0).astype(BF16)
    wt[...] = dot_nt(eye, w_ref[...]).astype(BF16).reshape(16, COLS, 1280)

    def w_lanes(k):
        return pl.ds(pl.multiple_of(lax.rem(lax.div(chip + 16 - k, 4), 4) * 1280, 128), 1280)

    def w_slot(k):
        return wbuf.at[lax.rem(chip + 16 - k, 4) * 2 + core, :, w_lanes(k)]

    wbuf[t, :, w_lanes(0)] = wt[chip]
    w_moved, w_handed = [], []

    def send_weights():
        for k in range(1, 16):
            w_moved.append(copies.start(wt.at[lax.rem(chip + k, 16)], w_slot(0), plane(k)))
        w_handed.append(copies.start(w_slot(0), w_slot(0), sibling))

    def hand_weights():
        for k in range(1, 16):
            w_moved[k - 1].wait_recv()
            w_handed.append(copies.start(w_slot(k), w_slot(k), sibling))

    lax.fori_loop(1, 32, wait_sums, 0)
    inverse = lax.rsqrt(jnp.sum(sums[...], axis=0) / WIDTH + EPSILON)
    slot = lax.broadcasted_iota(jnp.int32, (8, 128), 0) * 128 + lax.broadcasted_iota(jnp.int32, (8, 128), 1)
    live = (slot < len_ref[t]).astype(F32)
    scales[t, 0:4, :] = (inverse * live)[0:4]
    scaled = [copies.start(scales.at[t], scales.at[t], sibling)]
    for k in range(1, 4):
        scaled.append(copies.start(scales.at[t], scales.at[t], line(k, core)))
        scaled.append(copies.start(scales.at[t], scales.at[t], line(k, 1 - core)))
    send_weights()
    for k in range(1, 4):
        moved[k - 1].wait_recv()
        model = lax.rem(zl + 4 - k, 4) * 2 + core
        handed.append(copies.start(pieces.at[model], pieces.at[model], sibling))
    for copy in scaled + handed:
        copy.wait_recv()

    window = lax.rem(t, 4) * QUART
    shift = lax.broadcasted_iota(jnp.int32, (512, QUART), 0)
    shift = shift - lax.broadcasted_iota(jnp.int32, (512, QUART), 1)
    spread = lax.broadcasted_iota(jnp.int32, (80, 128), 0) == lax.broadcasted_iota(jnp.int32, (80, 128), 1)

    lane = lax.broadcasted_iota(jnp.int32, (80, 128), 1)

    def add_model(m, carry):
        acc, tile, first = carry
        size = len_ref[m]
        scale = scales[m]
        gain = jnp.where(mine == 0, scale[4:5], scale[5:6])
        gain = jnp.sum(jnp.where(spread, gain, 0.0), axis=1, keepdims=True)
        normed = (pieces[m].astype(F32) * row_of(scale) * gain).astype(BF16)
        pick = jnp.where(shift == window - first, 1.0, 0.0).astype(BF16)
        wide_normed = normed.astype(F32)
        total = jnp.sum(wide_normed * wide_normed, axis=1, keepdims=True)
        tile = jnp.where(lax.rem(lane, 8) == m, total, tile)
        return acc + dot(normed, pick), tile, first + size

    carry = (jnp.zeros((80, QUART), F32), jnp.zeros((80, 128), F32), jnp.int32(0))
    for m in range(MODELS):
        carry = add_model(m, carry)
    acc, tile, _ = carry
    high = tile.astype(BF16).astype(F32)
    middle = (tile - high).astype(BF16).astype(F32)
    tile = jnp.where(lane < 8, high, jnp.where(lane < 16, middle, tile - high - middle))
    tile = jnp.where(lane < 24, tile, 0.0)
    acc = jnp.concatenate([acc[:, :512], acc[:, 512:] + jnp.where(lax.rem(t, 4) == 3, tile, 0.0)], axis=1)
    lanes = pl.ds(pl.multiple_of(lax.rem(zl, 2) * QUART, 128), QUART)
    n_ref[x, zh, y, mine, :, :, lanes] = acc.astype(BF16).reshape(5, 16, QUART)

    def block_of(xx):
        return n_ref[xx].reshape(1280, LANES)

    def features(xx):
        return pl.ds(xx * 1280 if isinstance(xx, int) else pl.multiple_of(xx * 1280, 128), 1280)

    def each(body, init=0):
        for xx in range(4):
            init = body(xx, init)
        return init

    def fold_lanes(v):
        return functools.reduce(jnp.add, [v[:, 128 * k : 128 * k + 128] for k in range(10)])

    def swap_copy(slot, xx):
        return pltpu.make_async_remote_copy(
            src_ref=image.at[:, features(xx)],
            dst_ref=other.at[slot, :, features(xx)],
            send_sem=swap_send.at[slot * 4 + xx],
            recv_sem=swap_recv.at[slot * 4 + xx],
            device_id=sibling,
            device_id_type=MESH,
        )

    def norm_copy(step):
        return pltpu.make_async_remote_copy(
            src_ref=norm.at[step],
            dst_ref=other_norm.at[step],
            send_sem=norm_send.at[step],
            recv_sem=norm_recv.at[step],
            device_id=sibling,
            device_id_type=MESH,
        )

    def slots(first, count):
        at = lax.broadcasted_iota(jnp.int32, (1, count), 1) + first
        return at + core * QUART + jnp.where(at >= QUART, QUART, 0)

    take = lax.broadcasted_iota(jnp.int32, (16, 128), 1)
    take = (lax.rem(take, 8) == lax.broadcasted_iota(jnp.int32, (16, 128), 0)) & (take < 24)
    take = jnp.where(take, 1.0, 0.0).astype(BF16)

    def use_block(k, step):
        xx = lax.rem(x + k + 4, 4)
        if step == 0:
            spare = n_ref[xx, :, :, :, :, :, LANES - 128 :].reshape(1280, 128)
            sq[:, features(xx)] = dot_nt(take, spare)[:MODELS]
        weights = wbuf[:, :, features(xx)].reshape(MODELS * COLS, 1280)
        at = slice(CHUNK * step, CHUNK * step + CHUNK)
        block = n_ref[xx, :, :, :, :, :, at].reshape(1280, CHUNK)
        turned[xx, at, :] = block.T
        more = dot(weights, block)
        product[:, at] = more if k == 0 else product[:, at] + more

    def wait_weights():
        for copy in w_handed:
            copy.wait_recv()

    plan, whole = gather_plan(n_ref, t, x, c)
    first = [(8.0, [], hand_weights), (0.0, whole[0], wait_weights)]
    uses = [(1.0 * i, whole[k], functools.partial(use_block, k, i)) for k in (0, 1, -1, 2) for i in range(5)]
    sent = plan.run(copies, first + uses)
    sent += moved + handed + scaled
    swap_sq = copies.start(sq, other_sq, sibling)

    def right_part(xx, total):
        swap_copy(0, xx).wait_recv()
        part = features(xx)
        right = MIXING * (image[:, part] + other[0, :, part])
        squared = jnp.where(core == 1, sq[:, part], other_sq[:, part])
        for m in range(MODELS):
            right = right + (1.0 - MIXING) * squared[m : m + 1] * wbuf[m, :, part].astype(F32)
        diagonal[0:1, part] = (1.0 - MIXING) * jnp.sum(squared, axis=0, keepdims=True)
        direction[:, part] = right
        residual[:, part] = right
        d2[:, part] = split(right)
        length, inner = total
        return length + fold_lanes(right * right), inner + fold_lanes(diagonal[0:1, part] * right * right)

    def spread_out(v):
        return jnp.broadcast_to(jnp.sum(v, axis=1, keepdims=True), (COLS, 128))

    def block_copy(k, source, target, first):
        to = lax.rem(chip + k, 16)
        to = lax.div(to, 4) * 8 + lax.rem(to, 4) * 2 + core
        return pltpu.make_async_remote_copy(
            src_ref=source.at[to],
            dst_ref=target.at[chip],
            send_sem=out_send.at[first + k],
            recv_sem=out_recv.at[first + k],
            device_id=plane(k),
            device_id_type=MESH,
        )

    def send_blocks(values, source, target, first):
        def send_one(k, _):
            block_copy(k, source, target, first).start()
            return 0

        for group in range(8):
            value = values(pl.ds(640 * group, 640))
            for k in range(4):
                source[group * 4 + k, :, 0:160] = value[:, 160 * k : 160 * k + 160].astype(source.dtype)
        target[chip] = source[x * 8 + t]
        lax.fori_loop(1, 16, send_one, 0)

    def solve_step(step, _):
        @pl.when(step == 0)
        def _():
            slot = slots(0, LANES)
            outputs = jnp.zeros((COLS, LANES), F32)
            first = jnp.int32(0)
            for m in range(MODELS):
                size = len_ref[m]
                mask = jnp.where((slot >= first) & (slot < first + size), 1.0, 0.0)
                first = first + size
                outputs = outputs + mask * product[COLS * m : COLS * m + COLS, :]
            ub[:COLS] = outputs.astype(BF16)
            ub[COLS:] = jnp.zeros((COLS, LANES), BF16)

        @pl.when(step > 0)
        def _():
            total = jnp.zeros((2 * COLS, LANES), F32)
            for xx in range(4):
                total = total + dot(d2[:, 1280 * xx : 1280 * xx + 1280], block_of(xx))
            projected = fold(total) * jnp.where(slots(0, LANES) < LIVE, 1.0, 0.0)
            norm[step] = spread_out(fold_lanes(projected * projected))
            norm_copy(step).start()
            ub[...] = split(projected)

        @pl.when(step < ITERS)
        def _():
            for xx in range(5):
                if xx < 4:
                    image[:, 1280 * xx : 1280 * xx + 1280] = fold(dot(ub[...], turned[xx]))
                if xx > 0:
                    swap_copy(step, xx - 1).start()

        @pl.when(step == 0)
        def _():
            swap_sq.wait()
            zero = jnp.zeros((COLS, 128), F32)
            length, inner = each(right_part, (zero, zero))
            squared_norm[...], weighted[...] = spread_out(length), spread_out(inner)
            merged[...] = jnp.zeros_like(merged)

        @pl.when(step > 0)
        def _():
            norm_copy(step).wait()
            curvature = MIXING * (norm[step] + other_norm[step]) + weighted[...]
            size[...] = squared_norm[...] / curvature

        @pl.when((step > 0) & (step < ITERS))
        def _():
            factor = size[:, :1]
            merged[...] += factor * direction[...]

            @pl.when(step == ITERS - 1)
            def _():
                send_blocks(lambda part: merged[:, part], blocks, landed, 0)

            def residual_part(xx, total):
                part = features(xx)
                swap_copy(step, xx).wait_recv()
                full = MIXING * (image[:, part] + other[step, :, part]) + diagonal[0:1, part] * direction[:, part]
                rest = residual[:, part] - factor * full
                residual[:, part] = rest
                return total + fold_lanes(rest * rest)

            norm_next = spread_out(each(residual_part, jnp.zeros((COLS, 128), F32)))
            ratio = (norm_next / squared_norm[...])[:, :1]
            squared_norm[...] = norm_next

            def direction_part(xx, total):
                part = features(xx)
                now = residual[:, part] + ratio * direction[:, part]
                direction[:, part] = now
                d2[:, part] = split(now)
                return total + fold_lanes(diagonal[0:1, part] * now * now)

            weighted[...] = spread_out(each(direction_part, jnp.zeros((COLS, 128), F32)))

        @pl.when(step < ITERS)
        def _():
            def sent_part(xx, _):
                swap_copy(step, xx).wait_send()
                return 0

            each(sent_part)

        return 0

    lax.fori_loop(0, ITERS + 1, solve_step, 0)
    send_blocks(lambda part: size[:, :1] * direction[:, part], last_blocks, last_landed, 16)

    for copy in sent + w_moved + w_handed:
        copy.wait_send()
    lax.fori_loop(1, 32, wait_sums_sent, 0)

    def wait_blocks(k, _):
        block_copy(k, blocks, landed, 0).wait()
        block_copy(k, last_blocks, last_landed, 16).wait()
        return 0

    lax.fori_loop(1, 16, wait_blocks, 0)
    result = landed[...] + last_landed[...].astype(F32)
    out_ref[...] = result.reshape(256, 256).T[:160]


def body(hidden, gains, weights, lengths):
    vmem = pl.BlockSpec(memory_space=pltpu.VMEM)
    wide = (COLS, WIDTH)
    count = 250
    return pl.pallas_call(
        solve_kernel,
        out_shape=jax.ShapeDtypeStruct((160, 256), F32),
        in_specs=[vmem, vmem, vmem, pl.BlockSpec(memory_space=pltpu.SMEM)],
        out_specs=vmem,
        scratch_shapes=[
            pltpu.VMEM((32, 8, 128), F32),
            pltpu.VMEM((MODELS, 8, 128), F32),
            pltpu.VMEM((2, 80, 512), BF16),
            pltpu.VMEM((MODELS, 80, 512), BF16),
            pltpu.VMEM((16, COLS, 1280), BF16),
            pltpu.VMEM((4, 2, 4, 2, 5, 16, LANES), BF16),
            pltpu.VMEM((MODELS, COLS, WIDTH), BF16),
            pltpu.VMEM((2 * COLS, WIDTH), BF16),
            pltpu.VMEM(wide, F32),
            pltpu.VMEM((MODELS, WIDTH), F32),
            pltpu.VMEM((ITERS, COLS, WIDTH), F32),
            pltpu.VMEM((MODELS, WIDTH), F32),
            pltpu.VMEM((ITERS + 1, COLS, 128), F32),
            pltpu.VMEM((ITERS + 1, COLS, 128), F32),
            pltpu.VMEM(wide, F32),
            pltpu.VMEM(wide, F32),
            pltpu.VMEM(wide, F32),
            pltpu.VMEM((8, WIDTH), F32),
            pltpu.VMEM((COLS, 128), F32),
            pltpu.VMEM((COLS, 128), F32),
            pltpu.VMEM((COLS, 128), F32),
            pltpu.VMEM((2 * COLS, LANES), BF16),
            pltpu.VMEM((MODELS * COLS, LANES), F32),
            pltpu.VMEM((4, LANES, 1280), BF16),
            pltpu.VMEM((32, COLS, 256), F32),
            pltpu.VMEM((16, COLS, 256), F32),
            pltpu.VMEM((32, COLS, 256), BF16),
            pltpu.VMEM((16, COLS, 256), BF16),
            pltpu.SemaphoreType.DMA((32,)),
            pltpu.SemaphoreType.DMA((32,)),
            pltpu.SemaphoreType.DMA((4 * ITERS,)),
            pltpu.SemaphoreType.DMA((4 * ITERS,)),
            pltpu.SemaphoreType.DMA((ITERS + 1,)),
            pltpu.SemaphoreType.DMA((ITERS + 1,)),
            pltpu.SemaphoreType.DMA((32,)),
            pltpu.SemaphoreType.DMA((32,)),
            pltpu.SemaphoreType.DMA((count,)),
            pltpu.SemaphoreType.DMA((count,)),
        ],
        compiler_params=pltpu.CompilerParams(
            collective_id=0, has_side_effects=True, vmem_limit_bytes=56 * 2**20
        ),
    )(hidden.T, gains, weights[0], lengths)


def solution(mesh):
    return jax.shard_map(
        body,
        mesh=mesh,
        in_specs=(P("tok", ("row", "col")), P("tok", ("row", "col")), P("tok", "row", "col"), P()),
        out_specs=P(("row", "tok"), "col"),
        check_vma=False,
    )
```
